32 devices in a mesh: leaf: 8 (over z, x), rep: 4 (over y, core).
Axes of the slice: x: 2, y: 2, z: 4, core: 2. Of those that a mesh axis runs over, the one named last changes fastest.
Arguments:
- leaf_blocks: float32 [8192, 1024], P('leaf'), as said below
- generators: float32 [3, 128, 8192], P(None, 'rep', 'leaf'), may hold values from -0.5 to 0.5
- rhs: float32 [128, 8192], P('rep', 'leaf'), may hold values from -6 to 6
- order: int32 [8, 1024], P('leaf'), may hold values from 0 to 1023, each once within a row
- ranks: int32 [3, 8], P(None, 'leaf'), may hold values from 32 to 128, as said below
Outputs:
- solution: float32 [128, 8192], P('rep', 'leaf')
- determinants: float32 [4], replicated
The draws below stay inside these ranges and needn't reach their ends.
Inputs may be any that keep to these rules, and one draw needn't show every extreme that they name: `leaf_blocks`: each block of 1024 rows is a symmetric positive definite leaf covariance block. ranks[k, i] is equal for all leaves i of one depth-k node (equal i // 2**(k+1)); every level has a node of full rank 128. Each row of order is a permutation of the 1024 positions.
All inputs are finite; a program needn't handle non-finite values.
Results may differ from the reference program's by a relative error of at most 0.0003.
Values sent between devices are 32-bit elements; how exact they have to be, the bound alone decides.
No kernel may reach another device: no remote copies, remote signals or barrier semaphores. Data moves between devices by JAX's collectives and lax.ppermute only.
A program may use at most 128 MiB of HBM per device.

```python
import jax
import jax.numpy as jnp
from jax import lax

M = 1024
R = 128
NRHS = 128
LEAVES = 8
LEVELS = 3
N = 8192


length_scale = 0.1


noise_weight = 0.25


def matern_block(key, leaf):
    point_key, noise_key, nugget_key = jax.random.split(jax.random.fold_in(key, leaf + 101), 3)
    points = jax.random.uniform(point_key, (M, 2), jnp.float32, 0.0, 1.0)
    nugget = jax.random.uniform(nugget_key, (M,), jnp.float32, 0.4, 1.0)
    delta_x = points[:, 0][:, None] - points[:, 0][None, :]
    delta_y = points[:, 1][:, None] - points[:, 1][None, :]
    scaled = jnp.sqrt(3.0) * jnp.sqrt(delta_x * delta_x + delta_y * delta_y) / length_scale
    kernel = (1.0 + scaled) * jnp.exp(-scaled)
    uniform_draw = jax.random.uniform(noise_key, (M, M), jnp.float32, -1.0, 1.0)
    noise = 0.5 * (uniform_draw + uniform_draw.T) * (noise_weight / jnp.sqrt(jnp.float32(M)))
    identity = jnp.eye(M, dtype=jnp.float32)
    block = kernel + noise * (1.0 - identity) + identity * nugget[:, None]
    growth = 9.0 ** (leaf.astype(jnp.float32) / max(LEAVES - 1, 1))
    return block * growth


def draw_leaf_blocks(key, part):
    blocks = lax.map(lambda leaf: matern_block(key, leaf), jnp.arange(LEAVES, dtype=jnp.int32))
    return blocks.reshape(LEAVES * M, M)


def draw_ranks(key, part):
    leaf_index = jnp.arange(LEAVES, dtype=jnp.int32)
    per_level = []
    for depth in range(LEVELS):
        node_key, pick_key = jax.random.split(jax.random.fold_in(key, depth + 11))
        nodes = LEAVES // 2 ** (depth + 1)
        per_node = jax.random.randint(node_key, (nodes,), R // 4, R + 1, dtype=jnp.int32)
        chosen = jax.random.randint(pick_key, (), 0, nodes, dtype=jnp.int32)
        per_node = jnp.where(jnp.arange(nodes, dtype=jnp.int32) == chosen, R, per_node)
        per_level.append(per_node[leaf_index // 2 ** (depth + 1)])
    return jnp.stack(per_level).astype(jnp.int32)


def level_of(key, shape, cuts, least, high):
    def one(axis_at, blocks):
        steps = jax.random.uniform(jax.random.fold_in(jax.random.fold_in(key, 6), axis_at), (blocks,), jnp.float32, least / len(cuts), high / len(cuts))
        return jnp.repeat(jnp.exp(steps), shape[axis_at] // blocks).reshape((-1,) + (1,) * (len(shape) - axis_at - 1))

    gain = one(*cuts[0])
    for cut in cuts[1:]:
        gain = gain * one(*cut)
    return gain


def centred(own_key, extent, deviation, reach, pieces=(), kind=jnp.bfloat16):
    drawn = jax.random.normal(own_key, extent, jnp.float32) * deviation
    if len(pieces) > 0:
        drawn = level_of(own_key, extent, pieces, -0.22, 0.18) * drawn
    return jnp.clip(drawn, min=-reach, max=reach).astype(kind)


def setup_inputs(seed: int = 0) -> dict:
    arg_keys = jax.random.split(jax.random.key(seed), 6)
    leaf_blocks = draw_leaf_blocks(jax.random.fold_in(arg_keys[5], 71), 0)
    generators = centred(arg_keys[1], (LEVELS, R, N), R ** -0.5, 0.5, ((1, 4), (2, 8)), jnp.float32)
    rhs = centred(arg_keys[2], (NRHS, N), 1.0, 6.0, ((0, 4), (1, 8)), jnp.float32)
    order = jax.vmap(lambda own: jax.random.permutation(own, M))(jax.random.split(arg_keys[3], LEAVES)).reshape((LEAVES, M)).astype(jnp.int32)
    ranks = draw_ranks(jax.random.fold_in(arg_keys[5], 71), 0)
    return dict(leaf_blocks=leaf_blocks, generators=generators, rhs=rhs, order=order, ranks=ranks)


HIGHEST = lax.Precision.HIGHEST

def product(left, right):
    return jnp.dot(left.astype(jnp.float32), right.astype(jnp.float32), precision=HIGHEST, preferred_element_type=jnp.float32)

def solve_with(factor, values):
    return jax.scipy.linalg.cho_solve((factor, True), values)

def log_det(factor, count):
    return 2.0 * jnp.sum(jnp.log(jnp.diagonal(factor))) / count

def leaf_factor(inputs):
    block, stacked, tree_rhs = inputs
    factor = jnp.linalg.cholesky(block)
    gram_block = product(stacked, solve_with(factor, stacked.T))
    cross_block = product(stacked, solve_with(factor, tree_rhs.T))
    return (factor, jnp.concatenate([gram_block, cross_block], axis=1), log_det(factor, M))

def reference(leaf_blocks, generators, rhs, order, ranks):
    blocks = leaf_blocks.reshape(LEAVES, M, M)
    rank_index = lax.broadcasted_iota(jnp.int32, (LEVELS, R, LEAVES), 1)
    live = rank_index < ranks[:, None, :]
    masked = jnp.where(live[:, :, :, None], generators.reshape(LEVELS, R, LEAVES, M), 0.0)
    stacked = jnp.transpose(masked, (2, 0, 1, 3)).reshape(LEAVES, LEVELS * R, M)
    sensor = jnp.transpose(rhs.reshape(NRHS, LEAVES, M), (1, 0, 2))
    tree_rhs = jax.vmap(lambda values, index: jnp.take(values, index, axis=1))(sensor, order)
    factors, reduced, leaf_dets = lax.map(leaf_factor, (blocks, stacked, tree_rhs))
    batched_solve = jax.vmap(solve_with)
    identity = jnp.eye(R, dtype=jnp.float32)
    results = [jnp.mean(leaf_dets)]
    pivots = []
    for depth in range(LEVELS):
        merged = reduced[0::2] + reduced[1::2]
        pivot_rows = merged[:, :R]
        pivot_factor = jnp.linalg.cholesky(identity[None] + pivot_rows[:, :, :R])
        node_dets = 2.0 * jnp.sum(jnp.log(jnp.diagonal(pivot_factor, axis1=1, axis2=2)), axis=1) / R
        results.append(jnp.mean(node_dets))
        pivot_right = pivot_rows[:, :, R:]
        pivots.append((pivot_factor, pivot_right))
        lower_rows = merged[:, R:]
        reduced = lower_rows[:, :, R:] - jnp.einsum('nab,nbc->nac', lower_rows[:, :, :R], batched_solve(pivot_factor, pivot_right), precision=HIGHEST)
    coeffs = [None] * LEVELS
    for depth in reversed(range(LEVELS)):
        pivot_factor, pivot_right = pivots[depth]
        after = LEVELS - depth - 1
        target = pivot_right[:, :, after * R:]
        for ancestor in range(depth + 1, LEVELS):
            offset = (ancestor - depth - 1) * R
            parent = jnp.repeat(coeffs[ancestor], 2 ** (ancestor - depth), axis=0)
            target = target - jnp.einsum('nab,nbc->nac', pivot_right[:, :, offset:offset + R], parent, precision=HIGHEST)
        coeffs[depth] = batched_solve(pivot_factor, target)
    correction = jnp.transpose(tree_rhs, (0, 2, 1))
    for depth in range(LEVELS):
        per_leaf = jnp.repeat(coeffs[depth], 2 ** (depth + 1), axis=0)
        correction = correction - jnp.einsum('prm,prc->pmc', stacked[:, depth * R:(depth + 1) * R], per_leaf, precision=HIGHEST)
    solution_tree = batched_solve(factors, correction)
    placed = jax.vmap(lambda values, index: jnp.zeros_like(values).at[:, index].set(values))(jnp.transpose(solution_tree, (0, 2, 1)), order)
    solution = jnp.transpose(placed, (1, 0, 2)).reshape(NRHS, LEAVES * M)
    return (solution, jnp.stack(results))
```

```python
import functools

import jax
import jax.numpy as jnp
from jax import lax
from jax.experimental import pallas as pl
from jax.experimental.pallas import tpu as pltpu
from jax.sharding import PartitionSpec as P

F32 = jnp.float32
BF16 = jnp.bfloat16
B = 128
SUB = 8
PARAMS = pltpu.CompilerParams(vmem_limit_bytes=40 * 2**20)


def lanes_of(value, lane):
    index = jnp.full((SUB, B), lane, jnp.int32)
    return jnp.take_along_axis(value, index, axis=1, mode="promise_in_bounds")


def row_of(value, row):
    return jnp.broadcast_to(value[row : row + 1, :], (SUB, B))


def sweep(rows):
    lane = lax.broadcasted_iota(jnp.int32, (SUB, B), 1)
    sub = lax.broadcasted_iota(jnp.int32, (SUB, B), 0)
    count = B // SUB
    pivots = jnp.ones((SUB, B), F32)
    rows = list(rows)
    t, rt = [None] * count, [None] * count
    cols = [lanes_of(rows[0], l) for l in range(SUB)]
    for p in range(count):
        base = SUB * p
        inside = (lane >= base) & (lane < base + SUB)
        upto = lane < base + SUB
        panel = jnp.where(inside, jnp.where(lane - base == sub, 1.0, 0.0), rows[p])
        t[p] = jnp.where(upto, panel, 0.0)
        following = p + 1 < count
        ahead = None
        if following:
            first = [lanes_of(rows[p + 1], base + l) for l in range(SUB)]
            below = list(first)
            ahead = [lanes_of(rows[p + 1], base + SUB + l) for l in range(SUB)]
        for j in range(SUB):
            across = {l: row_of(cols[l], j) for l in range(j, SUB)}
            pivots = jnp.where(lane == base + j, across[j], pivots)
            inverse = pltpu.reciprocal(across[j], approx=True)
            scale = jnp.where(sub == j, 1.0 - inverse, cols[j] * inverse)
            for l in range(j + 1, SUB):
                cols[l] = cols[l] - scale * across[l]
            panel = panel - scale * row_of(panel, j)
            if following:
                factor = below[j] * inverse
                for l in range(SUB):
                    ahead[l] = ahead[l] - factor * row_of(below[j], l)
                for l in range(j + 1, SUB):
                    below[l] = below[l] - factor * across[l]
        rt[p] = jnp.where(upto, panel, 0.0)
        if following:
            spread = [row_of(panel, i) for i in range(SUB)]
        for q in range(p + 1, count):
            weight = first if q == p + 1 else [lanes_of(rows[q], base + l) for l in range(SUB)]
            even = jnp.where(inside, 0.0, rows[q]) - weight[0] * spread[0]
            odd = weight[1] * spread[1]
            for l in range(2, SUB, 2):
                even = even - weight[l] * spread[l]
                odd = odd + weight[l + 1] * spread[l + 1]
            rows[q] = even - odd
        cols = ahead
    return jnp.concatenate(t + rt, axis=0), pivots


def rows_from(ref):
    return [ref[SUB * p : SUB * (p + 1), :] for p in range(B // SUB)]


def split(value):
    high = value.astype(BF16)
    return high, (value - high.astype(F32)).astype(BF16)


def dot_nt(left, right):
    return lax.dot_general(left, right, (((1,), (1,)), ((), ())), preferred_element_type=F32)


def dot_nn(left, right):
    return lax.dot_general(left, right, (((1,), (0,)), ((), ())), preferred_element_type=F32)


def join(parts, axis):
    return jnp.concatenate(parts, axis=axis)


def product_nt(left, right):
    lh, ll = left
    rh, rl = right
    return dot_nt(join([lh, lh, ll], 1), join([rh, rl, rh], 1))


def product_nn(left, right):
    lh, ll = left
    rh, rl = right
    return dot_nn(join([lh, lh, ll], 1), join([rh, rl, rh], 0))


def log_sum(pivots):
    return jnp.sum(jnp.log(pivots[:1]), axis=1, keepdims=True)


def factor_kernel(
    blocks, low_hi, low_lo, tri_hi, tri_lo, logs, work, corner, mult_hi, mult_lo, sems
):
    points = work.shape[0]
    count = points // B
    whole_copy = pltpu.make_async_copy(blocks, work, sems.at[0])
    first_copy = pltpu.make_async_copy(blocks.at[:B, :B], corner, sems.at[1])
    first_copy.start()
    whole_copy.start()
    first_copy.wait()

    def step(k, total):
        tri, pivots = sweep(rows_from(corner))
        high, low = split(tri)
        tri_hi[k] = high
        tri_lo[k] = low

        for at in range(count - 1):

            @pl.when(k == at)
            def _():
                if at == 0:
                    whole_copy.wait()
                start, mid = at * B, (at + 1) * B
                both = product_nt(split(work[mid:, start:mid]), (tri_hi[at], tri_lo[at]))
                hi, lo = split(both[:, :B])
                low_hi[mid:, start:mid] = hi
                low_lo[mid:, start:mid] = lo
                hi, lo = split(both[:, B:])
                mult_hi[mid:, :] = hi
                mult_lo[mid:, :] = lo
                for col in range(mid, points, B):
                    change = product_nt(
                        (mult_hi[col:, :], mult_lo[col:, :]),
                        (
                            low_hi[col : col + B, start:mid],
                            low_lo[col : col + B, start:mid],
                        ),
                    )
                    fresh = work[col:, col : col + B] - change
                    work[col:, col : col + B] = fresh
                    if col == mid:
                        corner[...] = fresh[:B]

        return total + log_sum(pivots)

    total = lax.fori_loop(0, count, step, jnp.zeros((1, 1), F32))
    logs[...] = jnp.broadcast_to(total, logs.shape)


def factor_leaf(block):
    points = block.shape[1]
    count = points // B
    return pl.pallas_call(
        factor_kernel,
        out_shape=(
            jax.ShapeDtypeStruct((points, points), BF16),
            jax.ShapeDtypeStruct((points, points), BF16),
            jax.ShapeDtypeStruct((count, 2 * B, B), BF16),
            jax.ShapeDtypeStruct((count, 2 * B, B), BF16),
            jax.ShapeDtypeStruct((SUB, B), F32),
        ),
        in_specs=[pl.BlockSpec(memory_space=pl.ANY)],
        scratch_shapes=[
            pltpu.VMEM((points, points), F32),
            pltpu.VMEM((B, B), F32),
            pltpu.VMEM((points, B), BF16),
            pltpu.VMEM((points, B), BF16),
            pltpu.SemaphoreType.DMA((2,)),
        ],
        compiler_params=PARAMS,
        name="factor",
    )(block)


def permutation(order_ref, points):
    sensor = lax.broadcasted_iota(jnp.int32, (points, points), 0)
    return jnp.where(sensor == order_ref[...], 1.0, 0.0).astype(BF16)


def thirds(value):
    high = value.astype(BF16)
    rest = value - high.astype(F32)
    mid = rest.astype(BF16)
    return high, mid, (rest - mid.astype(F32)).astype(BF16)


def column_rows(levels, extra, entry):
    return (levels - entry) * B + extra


def forward_kernel(
    ranks, gathered, rhs, order, low_hi, low_lo, tri_hi, tri_lo, logs,
    message, w_hi, w_lo, perm, values, m_hi, m_lo,
):
    levels, _, points = gathered.shape
    extra = rhs.shape[0]
    count = points // B
    for level in range(levels):
        row = lax.broadcasted_iota(jnp.int32, (B, points), 0)
        values[level * B : (level + 1) * B, :] = jnp.where(
            row < ranks[level, 0], gathered[level], 0.0
        )
    perm[...] = permutation(order, points)
    moved = dot_nn(join(thirds(rhs[...]), 0), perm[...])
    values[levels * B :, :] = moved[:extra] + (moved[extra : 2 * extra] + moved[2 * extra :])
    for k in range(count):
        start, end = k * B, (k + 1) * B
        own = values[:, start:end]
        if k > 0:
            own = own - product_nt(
                (m_hi[:, :start], m_lo[:, :start]),
                (low_hi[start:end, :start], low_lo[start:end, :start]),
            )
        both = product_nt(split(own), (tri_hi[k], tri_lo[k]))
        hi, lo = split(both[:, :B])
        w_hi[:, start:end] = hi
        w_lo[:, start:end] = lo
        hi, lo = split(both[:, B:])
        m_hi[:, start:end] = hi
        m_lo[:, start:end] = lo
    at = 0
    for entry in range(levels):
        top = entry * B
        size = column_rows(levels, extra, entry)
        message[at : at + size, :] = product_nt(
            (m_hi[top:, :], m_lo[top:, :]), (w_hi[top : top + B, :], w_lo[top : top + B, :])
        )
        at += size
    lane = lax.broadcasted_iota(jnp.int32, (SUB, B), 1)
    message[at:, :] = jnp.where(lane == 0, logs[...] / points, 0.0)


def message_rows(levels, extra):
    return sum(column_rows(levels, extra, entry) for entry in range(levels)) + SUB


def vmem():
    return pl.BlockSpec(memory_space=pltpu.VMEM)


def forward(ranks, gathered, rhs, order, factors, logs):
    levels, _, points = gathered.shape
    extra = rhs.shape[0]
    rows = levels * B + extra
    return pl.pallas_call(
        forward_kernel,
        out_shape=(
            jax.ShapeDtypeStruct((message_rows(levels, extra), B), F32),
            jax.ShapeDtypeStruct((rows, points), BF16),
            jax.ShapeDtypeStruct((rows, points), BF16),
            jax.ShapeDtypeStruct((points, points), BF16),
        ),
        in_specs=[pl.BlockSpec(memory_space=pltpu.SMEM)] + [vmem()] * 8,
        out_specs=(vmem(),) * 4,
        scratch_shapes=[
            pltpu.VMEM((rows, points), F32),
            pltpu.VMEM((rows, points), BF16),
            pltpu.VMEM((rows, points), BF16),
        ],
        compiler_params=PARAMS,
        name="forward",
    )(ranks, gathered, rhs, order, *factors, logs)


def backward_kernel(low_hi, low_lo, tri_hi, tri_lo, w_hi, w_lo, perm, out, v_hi, v_lo, v_last):
    points = low_hi.shape[0]
    count = points // B
    for k in reversed(range(count)):
        start, end = k * B, (k + 1) * B
        own = w_hi[:, start:end].astype(F32) + w_lo[:, start:end].astype(F32)
        if end < points:
            own = own - product_nn(
                (v_hi[:, end:], v_lo[:, end:]), (low_hi[end:, start:end], low_lo[end:, start:end])
            )
        solved = product_nn(split(own), (tri_hi[k, B:, :], tri_lo[k, B:, :]))
        hi, mid, last = thirds(solved)
        v_hi[:, start:end] = hi
        v_lo[:, start:end] = mid
        v_last[:, start:end] = last
    sensors = perm[...]
    out[...] = dot_nt(v_hi[...], sensors) + (dot_nt(v_lo[...], sensors) + dot_nt(v_last[...], sensors))


def backward(factors, w_hi, w_lo, perm):
    rows, points = w_hi.shape
    return pl.pallas_call(
        backward_kernel,
        out_shape=jax.ShapeDtypeStruct((rows, points), F32),
        in_specs=[vmem()] * 7,
        out_specs=vmem(),
        scratch_shapes=[pltpu.VMEM((rows, points), BF16)] * 3,
        compiler_params=PARAMS,
        name="backward",
    )(*factors, w_hi, w_lo, perm)


def eliminate(depth, levels, extra, own, received, merged, corner):
    merged[...] = own[...] + received[...]
    size = column_rows(levels - depth, extra, 0)
    row = lax.broadcasted_iota(jnp.int32, (B, B), 0)
    column = lax.broadcasted_iota(jnp.int32, (B, B), 1)
    corner[...] = merged[:B, :] + jnp.where(row == column, 1.0, 0.0)
    tri, pivots = sweep(rows_from(corner))
    lane = lax.broadcasted_iota(jnp.int32, (SUB, B), 1)
    totals = merged[merged.shape[0] - SUB :, :] + jnp.where(
        lane == depth + 1, log_sum(pivots) / B, 0.0
    )
    pieces = split(tri)
    both = product_nt(split(merged[B:size, :]), pieces)
    return size, pieces, both, totals


def merge_kernel(depth, levels, own, received, message, w_out, tri_out, merged, corner):
    extra = w_out.shape[0] - (levels - depth - 1) * B
    size, pieces, both, totals = eliminate(
        depth, levels, extra, own, received, merged, corner
    )
    below = split(both[:, :B])
    mult = split(both[:, B:])
    w_out[...] = both[:, :B]
    tri_out[...] = pieces[0][B:].astype(F32) + pieces[1][B:].astype(F32)
    at = 0
    for entry in range(levels - depth - 1):
        top = entry * B
        rows = column_rows(levels - depth - 1, extra, entry)
        change = product_nt(
            tuple(part[top:] for part in mult), tuple(part[top : top + B] for part in below)
        )
        message[at : at + rows, :] = merged[size + at : size + at + rows, :] - change
        at += rows
    message[at:, :] = totals


def merge(depth, levels, extra, own, received):
    rows = column_rows(levels - depth, extra, 0) - B
    return pl.pallas_call(
        functools.partial(merge_kernel, depth, levels),
        out_shape=(
            jax.ShapeDtypeStruct((message_rows(levels - depth - 1, extra), B), F32),
            jax.ShapeDtypeStruct((rows, B), F32),
            jax.ShapeDtypeStruct((B, B), F32),
        ),
        in_specs=[vmem()] * 2,
        out_specs=(vmem(),) * 3,
        scratch_shapes=[pltpu.VMEM(own.shape, F32), pltpu.VMEM((B, B), F32)],
        compiler_params=PARAMS,
        name="merge",
    )(own, received)


def finish_kernel(levels, leaf_count, *refs):
    own, received, solved = refs[:3]
    saved = refs[3 : 3 + 2 * (levels - 1)]
    out, means, merged, corner = refs[3 + 2 * (levels - 1) :]
    extra = out.shape[0]
    depth = levels - 1
    _, pieces, both, totals = eliminate(depth, levels, extra, own, received, merged, corner)
    coeffs = [None] * levels
    coeffs[depth] = split(
        product_nn(split(both[:, :B]), tuple(part[B:] for part in pieces))
    )
    for level in reversed(range(levels - 1)):
        w_ref, tri_ref = saved[2 * level], saved[2 * level + 1]
        inner = (levels - level - 1) * B
        known = tuple(
            join([coeffs[m][part] for m in range(level + 1, levels)], 1) for part in range(2)
        )
        target = w_ref[inner:, :] - product_nn(known, split(w_ref[:inner, :]))
        coeffs[level] = split(product_nn(split(target), split(tri_ref[...])))
    known = tuple(join([coeffs[m][part] for m in range(levels)], 1) for part in range(2))
    out[...] = solved[levels * B :, :] - product_nn(known, split(solved[: levels * B, :]))
    lane = lax.broadcasted_iota(jnp.int32, (SUB, B), 1)
    scale = jnp.zeros((SUB, B), F32)
    for entry in range(levels + 1):
        scale = jnp.where(lane == entry, 2.0**entry / leaf_count, scale)
    means[...] = totals * scale


def finish(levels, leaf_count, extra, own, received, solved, saved):
    points = solved.shape[1]
    return pl.pallas_call(
        functools.partial(finish_kernel, levels, leaf_count),
        out_shape=(
            jax.ShapeDtypeStruct((extra, points), F32),
            jax.ShapeDtypeStruct((SUB, B), F32),
        ),
        in_specs=[vmem()] * (3 + len(saved)),
        out_specs=(vmem(),) * 2,
        scratch_shapes=[pltpu.VMEM(own.shape, F32), pltpu.VMEM((B, B), F32)],
        compiler_params=PARAMS,
        name="finish",
    )(own, received, solved, *saved)


def swapped(value, axis, bit):
    mask = 2**bit
    pairs = [(source, source ^ mask) for source in range(lax.axis_size(axis))]
    return lax.ppermute(value, axis, pairs)


def shards(leaf_blocks, generators, rhs, order, ranks):
    levels = generators.shape[0]
    extra = rhs.shape[0]
    gathered = lax.all_gather(generators, "rep", axis=1, tiled=True)
    *factors, logs = factor_leaf(leaf_blocks)
    message, w_hi, w_lo, perm = forward(ranks, gathered, rhs, order, factors, logs)
    saved = []
    for depth in range(levels - 1):
        received = swapped(message, "leaf", depth)
        if depth == 0:
            solved = backward(factors, w_hi, w_lo, perm)
        message, w_level, tri_level = merge(depth, levels, extra, message, received)
        saved += [w_level, tri_level]
    received = swapped(message, "leaf", levels - 1)
    out, means = finish(
        levels, lax.axis_size("leaf"), extra, message, received, solved, saved
    )
    return (out, means[0, : levels + 1])


def solution(mesh):
    placed = (
        P("leaf", None),
        P(None, "rep", "leaf"),
        P("rep", "leaf"),
        P("leaf", None),
        P(None, "leaf"),
    )
    return jax.shard_map(
        shards, mesh=mesh, in_specs=placed, out_specs=(P("rep", "leaf"), P()), check_vma=False
    )
```

```python
import functools

import jax
import jax.numpy as jnp
from jax import lax
from jax.experimental import pallas as pl
from jax.experimental.pallas import tpu as pltpu
from jax.sharding import PartitionSpec as P

F32 = jnp.float32
BF16 = jnp.bfloat16
B = 128
SUB = 8


def limit(mebibytes, flops=0):
    return dict(
        compiler_params=pltpu.CompilerParams(vmem_limit_bytes=mebibytes * 2**20),
        cost_estimate=pl.CostEstimate(flops=flops, bytes_accessed=2**20, transcendentals=0),
    )


def lanes_of(value, lane):
    index = jnp.full((SUB, B), lane, jnp.int32)
    return jnp.take_along_axis(value, index, axis=1, mode="promise_in_bounds")


def row_of(value, row):
    return jnp.broadcast_to(value[row : row + 1, :], (SUB, B))


def sweep(rows):
    lane = lax.broadcasted_iota(jnp.int32, (SUB, B), 1)
    sub = lax.broadcasted_iota(jnp.int32, (SUB, B), 0)
    count = B // SUB
    pivots = jnp.ones((SUB, B), F32)
    rows = list(rows)
    t, rt = [None] * count, [None] * count
    cols = [lanes_of(rows[0], l) for l in range(SUB)]
    for p in range(count):
        base = SUB * p
        inside = (lane >= base) & (lane < base + SUB)
        upto = lane < base + SUB
        panel = jnp.where(inside, jnp.where(lane - base == sub, 1.0, 0.0), rows[p])
        t[p] = jnp.where(upto, panel, 0.0)
        following = p + 1 < count
        ahead = None
        if following:
            first = [lanes_of(rows[p + 1], base + l) for l in range(SUB)]
            below = list(first)
            ahead = [lanes_of(rows[p + 1], base + SUB + l) for l in range(SUB)]
        for j in range(SUB):
            across = {l: row_of(cols[l], j) for l in range(j, SUB)}
            pivots = jnp.where(lane == base + j, across[j], pivots)
            inverse = pltpu.reciprocal(across[j], approx=True)
            scale = jnp.where(sub == j, 1.0 - inverse, cols[j] * inverse)
            for l in range(j + 1, SUB):
                cols[l] = cols[l] - scale * across[l]
            panel = panel - scale * row_of(panel, j)
            if following:
                factor = below[j] * inverse
                for l in range(SUB):
                    ahead[l] = ahead[l] - factor * row_of(below[j], l)
                for l in range(j + 1, SUB):
                    below[l] = below[l] - factor * across[l]
        rt[p] = jnp.where(upto, panel, 0.0)
        if following:
            spread = [row_of(panel, i) for i in range(SUB)]
        for q in range(p + 1, count):
            weight = first if q == p + 1 else [lanes_of(rows[q], base + l) for l in range(SUB)]
            even = jnp.where(inside, 0.0, rows[q]) - weight[0] * spread[0]
            odd = weight[1] * spread[1]
            for l in range(2, SUB, 2):
                even = even - weight[l] * spread[l]
                odd = odd + weight[l + 1] * spread[l + 1]
            rows[q] = even - odd
        cols = ahead
    return jnp.concatenate(t + rt, axis=0), pivots


def rows_from(ref):
    return [ref[SUB * p : SUB * (p + 1), :] for p in range(B // SUB)]


def split(value):
    high = value.astype(BF16)
    return high, (value - high.astype(F32)).astype(BF16)


def dot_nt(left, right):
    return lax.dot_general(left, right, (((1,), (1,)), ((), ())), preferred_element_type=F32)


def dot_nn(left, right):
    return lax.dot_general(left, right, (((1,), (0,)), ((), ())), preferred_element_type=F32)


def join(parts, axis):
    return jnp.concatenate(parts, axis=axis)


def product_nt(left, right):
    lh, ll = left
    rh, rl = right
    return dot_nt(join([lh, lh, ll], 1), join([rh, rl, rh], 1))


def product_nn(left, right):
    lh, ll = left
    rh, rl = right
    return dot_nn(join([lh, lh, ll], 1), join([rh, rl, rh], 0))


def log_sum(pivots):
    return jnp.sum(jnp.log(pivots[:1]), axis=1, keepdims=True)


def factor_kernel(
    blocks, low_hi, low_lo, tri_hi, tri_lo, logs, work, corner, mult_hi, mult_lo, sems
):
    points = work.shape[0]
    count = points // B
    whole_copy = pltpu.make_async_copy(blocks, work, sems.at[0])
    first_copy = pltpu.make_async_copy(blocks.at[:B, :B], corner, sems.at[1])
    first_copy.start()
    whole_copy.start()
    first_copy.wait()

    def step(k, total):
        tri, pivots = sweep(rows_from(corner))
        high, low = split(tri)
        tri_hi[k] = high
        tri_lo[k] = low

        for at in range(count - 1):

            @pl.when(k == at)
            def _():
                if at == 0:
                    whole_copy.wait()
                start, mid = at * B, (at + 1) * B
                both = product_nt(split(work[mid:, start:mid]), (tri_hi[at], tri_lo[at]))
                hi, lo = split(both[:, :B])
                low_hi[mid:, start:mid] = hi
                low_lo[mid:, start:mid] = lo
                hi, lo = split(both[:, B:])
                mult_hi[mid:, :] = hi
                mult_lo[mid:, :] = lo
                for col in range(mid, points, B):
                    change = product_nt(
                        (mult_hi[col:, :], mult_lo[col:, :]),
                        (
                            low_hi[col : col + B, start:mid],
                            low_lo[col : col + B, start:mid],
                        ),
                    )
                    fresh = work[col:, col : col + B] - change
                    work[col:, col : col + B] = fresh
                    if col == mid:
                        corner[...] = fresh[:B]

        return total + log_sum(pivots)

    total = lax.fori_loop(0, count, step, jnp.zeros((1, 1), F32))
    logs[...] = jnp.broadcast_to(total, logs.shape)


def vmem():
    return pl.BlockSpec(memory_space=pltpu.VMEM)


def factor_leaf(block):
    points = block.shape[1]
    count = points // B
    return pl.pallas_call(
        factor_kernel,
        out_shape=(
            jax.ShapeDtypeStruct((points, points), BF16),
            jax.ShapeDtypeStruct((points, points), BF16),
            jax.ShapeDtypeStruct((count, 2 * B, B), BF16),
            jax.ShapeDtypeStruct((count, 2 * B, B), BF16),
            jax.ShapeDtypeStruct((SUB, B), F32),
        ),
        in_specs=[pl.BlockSpec(memory_space=pltpu.HBM)],
        out_specs=(vmem(),) * 5,
        scratch_shapes=[
            pltpu.VMEM((points, points), F32),
            pltpu.VMEM((B, B), F32),
            pltpu.VMEM((points, B), BF16),
            pltpu.VMEM((points, B), BF16),
            pltpu.SemaphoreType.DMA((2,)),
        ],
        **limit(10),
        name="factor",
    )(block)


def permutation(order_ref, points):
    sensor = lax.broadcasted_iota(jnp.int32, (points, points), 0)
    return jnp.where(sensor == order_ref[...], 1.0, 0.0).astype(BF16)


def thirds(value):
    high = value.astype(BF16)
    rest = value - high.astype(F32)
    mid = rest.astype(BF16)
    return high, mid, (rest - mid.astype(F32)).astype(BF16)


def column_rows(levels, extra, entry):
    return (levels - entry) * B + extra


def halves(levels):
    shared = sum((levels - entry) * B for entry in range(levels))
    return shared, shared // 2 if levels > 1 else shared


def forward_kernel(levels, size, *refs):
    ranks, *pieces = refs[: size + 1]
    rhs, order, low_hi, low_lo, tri_hi, tri_lo, logs = refs[size + 1 : size + 8]
    shared, tail, send, w_hi, w_lo, perm, values, m_hi, m_lo = refs[size + 8 :]
    points = rhs.shape[1]
    extra = rhs.shape[0]
    count = points // B
    quarter = pieces[0].shape[1]
    own = lax.axis_index("rep")
    for level in range(levels):
        limit_here = ranks[:, level : level + 1]
        for shift in range(size):
            first = (own ^ shift) * quarter
            row = lax.broadcasted_iota(jnp.int32, (quarter, points), 0) + first
            at = pl.multiple_of(level * B + first, SUB)
            values[pl.ds(at, quarter), :] = jnp.where(
                row < limit_here, pieces[shift][level], 0.0
            )
    perm[...] = permutation(order, points)
    moved = dot_nn(join(thirds(rhs[...]), 0), perm[...])
    values[levels * B :, :] = moved[:extra] + (moved[extra : 2 * extra] + moved[2 * extra :])
    for k in range(count):
        start, end = k * B, (k + 1) * B
        here = values[:, start:end]
        if k > 0:
            here = here - product_nt(
                (m_hi[:, :start], m_lo[:, :start]),
                (low_hi[start:end, :start], low_lo[start:end, :start]),
            )
        both = product_nt(split(here), (tri_hi[k], tri_lo[k]))
        hi, lo = split(both[:, :B])
        w_hi[:, start:end] = hi
        w_lo[:, start:end] = lo
        hi, lo = split(both[:, B:])
        m_hi[:, start:end] = hi
        m_lo[:, start:end] = lo
    at = 0
    for entry in range(levels):
        top = entry * B
        rows = (levels - entry) * B
        block = product_nt(
            (m_hi[top:, :], m_lo[top:, :]), (w_hi[top : top + B, :], w_lo[top : top + B, :])
        )
        shared[at : at + rows, :] = block[:rows]
        tail[entry * extra : (entry + 1) * extra, :] = block[rows:]
        at += rows
    lane = lax.broadcasted_iota(jnp.int32, (SUB, B), 1)
    tail[levels * extra :, :] = jnp.where(lane == 0, logs[...] / points, 0.0)
    outgoing(shared, tail, send)


def outgoing(shared, tail, send):
    half = send.shape[0] - tail.shape[0]
    if half == shared.shape[0]:
        send[:half, :] = shared[...]
    else:
        start = pl.multiple_of((lax.axis_index("rep") % 2) * half, SUB)
        send[:half, :] = shared[pl.ds(start, half), :]
    send[half:, :] = tail[...]


def message_shapes(levels, extra):
    shared, half = halves(levels)
    tail = levels * extra + SUB
    return [jax.ShapeDtypeStruct((rows, B), F32) for rows in (shared, tail, half + tail)]


def forward(ranks, pieces, rhs, order, factors, logs):
    levels, _, points = pieces[0].shape
    extra = rhs.shape[0]
    rows = levels * B + extra
    return pl.pallas_call(
        functools.partial(forward_kernel, levels, len(pieces)),
        out_shape=(
            *message_shapes(levels, extra),
            jax.ShapeDtypeStruct((rows, points), BF16),
            jax.ShapeDtypeStruct((rows, points), BF16),
            jax.ShapeDtypeStruct((points, points), BF16),
        ),
        in_specs=[vmem()] * (8 + len(pieces)),
        out_specs=(vmem(),) * 6,
        scratch_shapes=[
            pltpu.VMEM((rows, points), F32),
            pltpu.VMEM((rows, points), BF16),
            pltpu.VMEM((rows, points), BF16),
        ],
        **limit(12),
        name="forward",
    )(ranks, *pieces, rhs, order, *factors, logs)


def backward_kernel(low_hi, low_lo, tri_hi, tri_lo, w_hi, w_lo, v_hi, v_mid, v_last):
    points = low_hi.shape[0]
    count = points // B
    for k in reversed(range(count)):
        start, end = k * B, (k + 1) * B
        own = w_hi[:, start:end].astype(F32) + w_lo[:, start:end].astype(F32)
        if end < points:
            own = own - product_nn(
                (v_hi[:, end:], v_mid[:, end:]),
                (low_hi[end:, start:end], low_lo[end:, start:end]),
            )
        solved = product_nn(split(own), (tri_hi[k, B:, :], tri_lo[k, B:, :]))
        hi, mid, last = thirds(solved)
        v_hi[:, start:end] = hi
        v_mid[:, start:end] = mid
        v_last[:, start:end] = last


def backward(factors, w_hi, w_lo):
    return pl.pallas_call(
        backward_kernel,
        out_shape=(jax.ShapeDtypeStruct(w_hi.shape, BF16),) * 3,
        in_specs=[vmem()] * 6,
        out_specs=(vmem(),) * 3,
        **limit(8, 4 * 10**9),
        name="backward",
    )(*factors, w_hi, w_lo)


def unorder_kernel(v_hi, v_mid, v_last, perm, out):
    sensors = perm[...]
    out[...] = dot_nt(v_hi[...], sensors) + (dot_nt(v_mid[...], sensors) + dot_nt(v_last[...], sensors))


def unorder(solved, perm):
    return pl.pallas_call(
        unorder_kernel,
        out_shape=jax.ShapeDtypeStruct(solved[0].shape, F32),
        in_specs=[vmem()] * 4,
        out_specs=vmem(),
        **limit(12, 4 * 10**9),
        name="unorder",
    )(*solved, perm)


def eliminate(depth, levels, extra, refs):
    shared, tail, received, *other, merged, below, corner = refs
    left = levels - depth
    whole, half = halves(left)
    if other:
        start = pl.multiple_of((lax.axis_index("rep") % 2) * half, SUB)
        across = pl.multiple_of(half - start, SUB)
        merged[pl.ds(start, half), :] = shared[pl.ds(start, half), :] + received[:half, :]
        merged[pl.ds(across, half), :] = shared[pl.ds(across, half), :] + other[0][...]
    else:
        merged[...] = shared[...] + received[:half, :]
    below[...] = tail[...] + received[half:, :]
    row = lax.broadcasted_iota(jnp.int32, (B, B), 0)
    column = lax.broadcasted_iota(jnp.int32, (B, B), 1)
    corner[...] = merged[:B, :] + jnp.where(row == column, 1.0, 0.0)
    tri, pivots = sweep(rows_from(corner))
    lane = lax.broadcasted_iota(jnp.int32, (SUB, B), 1)
    totals = below[left * extra :, :] + jnp.where(
        lane == depth + 1, log_sum(pivots) / B, 0.0
    )
    pieces = split(tri)
    panel = join([merged[B : left * B, :], below[:extra, :]], 0) if left > 1 else below[:extra, :]
    both = product_nt(split(panel), pieces)
    return pieces, both, totals


def merge_kernel(depth, levels, extra, *refs):
    inputs = refs[:4]
    next_shared, next_tail, send, w_out, tri_out = refs[4:9]
    scratch = refs[9:]
    merged, below = scratch[:2]
    pieces, both, totals = eliminate(depth, levels, extra, inputs + scratch)
    left = levels - depth - 1
    w_parts = split(both[:, :B])
    m_parts = split(both[:, B:])
    w_out[...] = both[:, :B]
    tri_out[...] = pieces[0][B:].astype(F32) + pieces[1][B:].astype(F32)
    at = 0
    for entry in range(left):
        top = entry * B
        rows = (left - entry) * B
        change = product_nt(
            tuple(part[top:] for part in m_parts),
            tuple(part[top : top + B] for part in w_parts),
        )
        base = (left + 1) * B + at
        next_shared[at : at + rows, :] = merged[base : base + rows, :] - change[:rows]
        next_tail[entry * extra : (entry + 1) * extra, :] = (
            below[(entry + 1) * extra : (entry + 2) * extra, :] - change[rows:]
        )
        at += rows
    next_tail[left * extra :, :] = totals
    outgoing(next_shared, next_tail, send)


def scratch_for(levels, extra):
    shared, tail, _ = message_shapes(levels, extra)
    return [
        pltpu.VMEM(shared.shape, F32),
        pltpu.VMEM(tail.shape, F32),
        pltpu.VMEM((B, B), F32),
    ]


def merge(depth, levels, extra, message):
    left = levels - depth
    return pl.pallas_call(
        functools.partial(merge_kernel, depth, levels, extra),
        out_shape=(
            *message_shapes(left - 1, extra),
            jax.ShapeDtypeStruct(((left - 1) * B + extra, B), F32),
            jax.ShapeDtypeStruct((B, B), F32),
        ),
        in_specs=[vmem()] * 4,
        out_specs=(vmem(),) * 5,
        scratch_shapes=scratch_for(left, extra),
        **limit(6),
        name="merge",
    )(*message)


def finish_kernel(levels, leaf_count, *refs):
    solved = refs[3]
    last = 4 + 2 * (levels - 1)
    saved = refs[4:last]
    out, means = refs[last : last + 2]
    extra = out.shape[0]
    depth = levels - 1
    pieces, both, totals = eliminate(depth, levels, extra, refs[:3] + refs[last + 2 :])
    coeffs = [None] * levels
    coeffs[depth] = split(
        product_nn(split(both[:, :B]), tuple(part[B:] for part in pieces))
    )
    for level in reversed(range(levels - 1)):
        w_ref, tri_ref = saved[2 * level], saved[2 * level + 1]
        inner = (levels - level - 1) * B
        known = tuple(
            join([coeffs[m][part] for m in range(level + 1, levels)], 1) for part in range(2)
        )
        target = w_ref[inner:, :] - product_nn(known, split(w_ref[:inner, :]))
        coeffs[level] = split(product_nn(split(target), split(tri_ref[...])))
    known = tuple(join([coeffs[m][part] for m in range(levels)], 1) for part in range(2))
    out[...] = solved[levels * B :, :] - product_nn(known, split(solved[: levels * B, :]))
    lane = lax.broadcasted_iota(jnp.int32, (SUB, B), 1)
    scale = jnp.zeros((SUB, B), F32)
    for entry in range(levels + 1):
        scale = jnp.where(lane == entry, 2.0**entry / leaf_count, scale)
    means[...] = (totals * scale)[:1, : levels + 1]


def finish(levels, leaf_count, extra, message, solved, saved):
    points = solved.shape[1]
    return pl.pallas_call(
        functools.partial(finish_kernel, levels, leaf_count),
        out_shape=(
            jax.ShapeDtypeStruct((extra, points), F32),
            jax.ShapeDtypeStruct((1, levels + 1), F32),
        ),
        in_specs=[vmem()] * (4 + len(saved)),
        out_specs=(vmem(),) * 2,
        scratch_shapes=scratch_for(1, extra),
        **limit(6),
        name="finish",
    )(*message, solved, *saved)


def swapped(value, axis, mask):
    pairs = [(source, source ^ mask) for source in range(lax.axis_size(axis))]
    return lax.ppermute(value, axis, pairs)


def exchange(message, depth, left, meanwhile=None):
    shared, tail, send = message
    received = swapped(send, "leaf", 2**depth)
    done = None
    if meanwhile is not None:
        received, done = lax.optimization_barrier((received, meanwhile()))
    if send.shape[0] == shared.shape[0] + tail.shape[0]:
        return (shared, tail, received), done
    other = swapped(received[: halves(left)[1]], "rep", 1)
    return (shared, tail, received, other), done


def shards(leaf_blocks, generators, rhs, order, ranks):
    levels = generators.shape[0]
    extra = rhs.shape[0]
    pieces = [generators]
    pieces += [swapped(generators, "rep", shift) for shift in range(1, lax.axis_size("rep"))]
    leaf_blocks = pltpu.with_memory_space_constraint(leaf_blocks, pltpu.HBM)
    *factors, logs = factor_leaf(leaf_blocks)
    *message, w_hi, w_lo, perm = forward(ranks.T, pieces, rhs, order, factors, logs)
    saved, solved = [], None
    jobs = [lambda: backward(factors, w_hi, w_lo), lambda: unorder(solved, perm)]
    for depth in range(levels - 1):
        arrived, done = exchange(message, depth, levels - depth, jobs.pop(0) if jobs else None)
        solved = solved if done is None else done
        *message, w_level, tri_level = merge(depth, levels, extra, arrived)
        saved += [w_level, tri_level]
    arrived, _ = exchange(message, levels - 1, 1)
    out, means = finish(levels, lax.axis_size("leaf"), extra, arrived, solved, saved)
    return (out, means.reshape(levels + 1))


def solution(mesh):
    placed = (
        P("leaf", None),
        P(None, "rep", "leaf"),
        P("rep", "leaf"),
        P("leaf", None),
        P(None, "leaf"),
    )
    return jax.shard_map(
        shards, mesh=mesh, in_specs=placed, out_specs=(P("rep", "leaf"), P()), check_vma=False
    )
```

```python
import functools

import jax
import jax.numpy as jnp
from jax import lax
from jax.experimental import pallas as pl
from jax.experimental.pallas import tpu as pltpu
from jax.sharding import PartitionSpec as P

F32 = jnp.float32
BF16 = jnp.bfloat16
B = 128
SUB = 8


def limit(mebibytes, flops=0):
    return dict(
        compiler_params=pltpu.CompilerParams(vmem_limit_bytes=mebibytes * 2**20),
        cost_estimate=pl.CostEstimate(flops=flops, bytes_accessed=2**20, transcendentals=0),
    )


def vmem():
    return pl.BlockSpec(memory_space=pltpu.VMEM)


def lanes_of(value, lane):
    index = jnp.full((SUB, B), lane, jnp.int32)
    return jnp.take_along_axis(value, index, axis=1, mode="promise_in_bounds")


def row_of(value, row):
    return jnp.broadcast_to(value[row : row + 1, :], (SUB, B))


def sweep(rows):
    lane = lax.broadcasted_iota(jnp.int32, (SUB, B), 1)
    sub = lax.broadcasted_iota(jnp.int32, (SUB, B), 0)
    count = B // SUB
    pivots = jnp.ones((SUB, B), F32)
    rows = list(rows)
    t, rt = [None] * count, [None] * count
    cols = [lanes_of(rows[0], l) for l in range(SUB)]
    for p in range(count):
        base = SUB * p
        inside = (lane >= base) & (lane < base + SUB)
        upto = lane < base + SUB
        panel = jnp.where(inside, jnp.where(lane - base == sub, 1.0, 0.0), rows[p])
        t[p] = jnp.where(upto, panel, 0.0)
        following = p + 1 < count
        ahead = None
        if following:
            first = [lanes_of(rows[p + 1], base + l) for l in range(SUB)]
            below = list(first)
            ahead = [lanes_of(rows[p + 1], base + SUB + l) for l in range(SUB)]
        for j in range(SUB):
            across = {l: row_of(cols[l], j) for l in range(j, SUB)}
            pivots = jnp.where(lane == base + j, across[j], pivots)
            inverse = pltpu.reciprocal(across[j], approx=True)
            scale = jnp.where(sub == j, 1.0 - inverse, cols[j] * inverse)
            for l in range(j + 1, SUB):
                cols[l] = cols[l] - scale * across[l]
            panel = panel - scale * row_of(panel, j)
            if following:
                factor = below[j] * inverse
                for l in range(SUB):
                    ahead[l] = ahead[l] - factor * row_of(below[j], l)
                for l in range(j + 1, SUB):
                    below[l] = below[l] - factor * across[l]
        rt[p] = jnp.where(upto, panel, 0.0)
        if following:
            spread = [row_of(panel, i) for i in range(SUB)]
        for q in range(p + 1, count):
            weight = first if q == p + 1 else [lanes_of(rows[q], base + l) for l in range(SUB)]
            even = jnp.where(inside, 0.0, rows[q]) - weight[0] * spread[0]
            odd = weight[1] * spread[1]
            for l in range(2, SUB, 2):
                even = even - weight[l] * spread[l]
                odd = odd + weight[l + 1] * spread[l + 1]
            rows[q] = even - odd
        cols = ahead
    return jnp.concatenate(t + rt, axis=0), pivots


def rows_from(ref):
    return [ref[SUB * p : SUB * (p + 1), :B] for p in range(B // SUB)]


def split(value):
    high = value.astype(BF16)
    return high, (value - high.astype(F32)).astype(BF16)


def dot_nt(left, right):
    return lax.dot_general(left, right, (((1,), (1,)), ((), ())), preferred_element_type=F32)


def dot_nn(left, right):
    return lax.dot_general(left, right, (((1,), (0,)), ((), ())), preferred_element_type=F32)


def join(parts, axis):
    return jnp.concatenate(parts, axis=axis)


def product_nt(left, right):
    lh, ll = left
    rh, rl = right
    return dot_nt(join([lh, lh, ll], 1), join([rh, rl, rh], 1))


def product_nn(left, right):
    lh, ll = left
    rh, rl = right
    return dot_nn(join([lh, lh, ll], 1), join([rh, rl, rh], 0))


def log_sum(pivots):
    return jnp.sum(jnp.log(pivots[:1]), axis=1, keepdims=True)


def below_of(low, first, at, top, bottom):
    skip = (first + 1) * B
    left = (at - first) * B
    return tuple(ref[top - skip : bottom - skip, left : left + B] for ref in low)


def factor_block(at, first, rows, pending, source, target, low, tri_refs, ready=None):
    (src, src_off), (dst, dst_off) = source, target
    points = src.shape[0] + src_off
    tri, pivots = sweep(rows)
    if ready is not None:
        ready()
    tri = split(tri)
    for ref, part in zip(tri_refs, tri):
        ref[at - first] = part
    start, mid = at * B, (at + 1) * B
    if mid == points:
        return None, None, log_sum(pivots)

    def current(top, col):
        fresh = src[top - src_off :, col - src_off : col - src_off + B]
        if pending is None:
            return fresh
        mult, below = pending
        return fresh - product_nt(
            tuple(part[top - start :] for part in mult),
            tuple(part[col - start : col - start + B] for part in below),
        )

    panel = current(mid, start)
    corner = None
    for col in range(mid, points, B):
        if pending is not None:
            dst[col - dst_off :, col - dst_off : col - dst_off + B] = current(col, col)
    corner = dst if pending is not None else src
    corner_off = mid - (dst_off if pending is not None else src_off)
    corner = corner[corner_off : corner_off + B, corner_off : corner_off + B]
    both = product_nt(split(panel[:B]), tri)
    below, mult = split(both[:, :B]), split(both[:, B:])
    corner = corner - product_nt(mult, below)
    if mid + B < points:
        both = product_nt(split(panel[B:]), tri)
        below = tuple(join(pair, 0) for pair in zip(below, split(both[:, :B])))
        mult = tuple(join(pair, 0) for pair in zip(mult, split(both[:, B:])))
    left = start - first * B
    for ref, part in zip(low, below):
        ref[mid - (first + 1) * B :, left : left + B] = part
    following = [corner[SUB * p : SUB * (p + 1)] for p in range(B // SUB)]
    return following, (mult, below), log_sum(pivots)


def hand_on(rows, pending, total, corner, mult_hi, mult_lo, logs):
    for p, row in enumerate(rows):
        corner[SUB * p : SUB * (p + 1), :] = row
    mult_hi[...], mult_lo[...] = pending[0]
    logs[...] = jnp.broadcast_to(total, logs.shape)


def head_kernel(
    first, last, blocks, low_hi, low_lo, tri_hi, tri_lo,
    logs, next_corner, mult_hi, mult_lo, work, corner, sems,
):
    whole_copy = pltpu.make_async_copy(blocks, work, sems.at[0])
    first_copy = pltpu.make_async_copy(blocks.at[:B, :B], corner, sems.at[1])
    first_copy.start()
    whole_copy.start()
    first_copy.wait()
    rows, pending = rows_from(corner), None
    total = jnp.zeros((1, 1), F32)
    for at in range(first, last):
        rows, pending, part = factor_block(
            at, first, rows, pending, (work, 0), (work, 0), (low_hi, low_lo),
            (tri_hi, tri_lo), whole_copy.wait if at == 0 else None,
        )
        total = total + part
    hand_on(rows, pending, total, next_corner, mult_hi, mult_lo, logs)


def resume(first, mult, low):
    left = low[0].shape[1] - B
    rows = mult[0].shape[0]
    below = tuple(ref[low[0].shape[0] - rows :, left:] for ref in low)
    return tuple(ref[...] for ref in mult), below


def middle_kernel(
    first, last, old_hi, old_lo, logs_before, corner, old_mult_hi, old_mult_lo, before,
    low_hi, low_lo, tri_hi, tri_lo, logs, next_corner, mult_hi, mult_lo, rest, work,
):
    rows = rows_from(corner)
    pending = resume(first, (old_mult_hi, old_mult_lo), (old_hi, old_lo))
    total = logs_before[:1, :1]
    for at in range(first, last):
        source = (before, 0) if at == first else (work, first * B)
        target = (rest, last * B) if at + 1 == last else (work, first * B)
        rows, pending, part = factor_block(
            at, first, rows, pending, source, target, (low_hi, low_lo), (tri_hi, tri_lo)
        )
        total = total + part
    hand_on(rows, pending, total, next_corner, mult_hi, mult_lo, logs)


def segment_shapes(first, last, points):
    low = ((points // B - first - 1) * B, (last - first) * B)
    tri = (last - first, 2 * B, B)
    return [jax.ShapeDtypeStruct(shape, BF16) for shape in (low, low, tri, tri)]


def factor_shapes(first, last, points):
    left = points - last * B
    held = points if first == 0 else left
    return (
        *segment_shapes(first, last, points),
        jax.ShapeDtypeStruct((SUB, B), F32),
        jax.ShapeDtypeStruct((B, B), F32),
        jax.ShapeDtypeStruct((left, B), BF16),
        jax.ShapeDtypeStruct((left, B), BF16),
        jax.ShapeDtypeStruct((held, held), F32),
    )


def head(first, last, block):
    points = block.shape[1]
    return pl.pallas_call(
        functools.partial(head_kernel, first, last),
        out_shape=factor_shapes(first, last, points),
        in_specs=[pl.BlockSpec(memory_space=pltpu.HBM)],
        out_specs=(vmem(),) * 9,
        scratch_shapes=[pltpu.VMEM((B, B), F32), pltpu.SemaphoreType.DMA((2,))],
        **limit(10),
        name="head",
    )(pltpu.with_memory_space_constraint(block, pltpu.HBM))


def middle(first, last, points, low, state):
    return pl.pallas_call(
        functools.partial(middle_kernel, first, last),
        out_shape=factor_shapes(first, last, points),
        in_specs=[vmem()] * 7,
        out_specs=(vmem(),) * 9,
        scratch_shapes=[pltpu.VMEM((points - first * B,) * 2, F32)],
        **limit(10),
        name="middle",
    )(*low, *state)


def permutation(order_ref, points):
    sensor = lax.broadcasted_iota(jnp.int32, (points, points), 0)
    return jnp.where(sensor == order_ref[...], 1.0, 0.0).astype(BF16)


def thirds(value):
    high = value.astype(BF16)
    rest = value - high.astype(F32)
    mid = rest.astype(BF16)
    return high, mid, (rest - mid.astype(F32)).astype(BF16)


def column_rows(levels, extra, entry):
    return (levels - entry) * B + extra


def halves(levels):
    shared = sum((levels - entry) * B for entry in range(levels))
    return shared, shared // 2 if levels > 1 else shared


def gram_tiles(levels, extra):
    bottom = levels * B + extra
    tiles = []
    for entry in range(0, levels, 2):
        left, mid, right = entry * B, (entry + 1) * B, (entry + 2) * B
        if entry + 1 < levels:
            tiles += [(left, mid, left, mid), (mid, bottom, left, right)]
        else:
            tiles.append((left, bottom, left, mid))
    return tiles


def forward_kernel(levels, size, segments, *refs):
    refs = list(refs)

    def take(number):
        taken = refs[:number]
        del refs[:number]
        return taken

    logs, corner, mult_hi, mult_lo, before, ranks = take(6)
    parts = [take(4) for _ in segments[:-1]]
    pieces = take(size)
    rhs, order, shared, tail, send, w_hi, w_lo, perm = take(8)
    parts.append(take(4))
    work, values, m_hi, m_lo = refs
    points = rhs.shape[1]
    extra = rhs.shape[0]
    count = points // B
    quarter = pieces[0].shape[1]
    own = lax.axis_index("rep")
    for level in range(levels):
        limit_here = ranks[:, level : level + 1]
        for shift in range(size):
            first = (own ^ shift) * quarter
            row = lax.broadcasted_iota(jnp.int32, (quarter, points), 0) + first
            at = pl.multiple_of(level * B + first, SUB)
            values[pl.ds(at, quarter), :] = jnp.where(
                row < limit_here, pieces[shift][level], 0.0
            )
    perm[...] = permutation(order, points)
    moved = dot_nn(join(thirds(rhs[...]), 0), perm[...])
    values[levels * B :, :] = moved[:extra] + (moved[extra : 2 * extra] + moved[2 * extra :])

    def advance(k):
        start, end = k * B, (k + 1) * B
        here = values[:, start:end]
        for (low_hi, low_lo, _, _), (first, last) in zip(parts, segments):
            stop = min(last, k)
            for left, right in ((first, min(stop, k - 1)), (max(first, k - 1), stop)):
                if left < right:
                    rows = slice(start - (first + 1) * B, end - (first + 1) * B)
                    columns = slice((left - first) * B, (right - first) * B)
                    held = slice(left * B, right * B)
                    here = here - product_nt(
                        (m_hi[:, held], m_lo[:, held]),
                        (low_hi[rows, columns], low_lo[rows, columns]),
                    )
        for (_, _, tri_hi, tri_lo), (first, last) in zip(parts, segments):
            if first <= k < last:
                both = product_nt(split(here), (tri_hi[k - first], tri_lo[k - first]))
        hi, lo = split(both[:, :B])
        w_hi[:, start:end] = hi
        w_lo[:, start:end] = lo
        hi, lo = split(both[:, B:])
        m_hi[:, start:end] = hi
        m_lo[:, start:end] = lo

    first, last = segments[-1]
    low_hi, low_lo, tri_hi, tri_lo = parts[-1]
    rows = rows_from(corner)
    pending = resume(first, (mult_hi, mult_lo), parts[-2][:2])
    total = logs[:1, :1]
    tiles = gram_tiles(levels, extra)
    sums = [None] * len(tiles)
    done, summed = 0, 0

    def accumulate(stop):
        held = slice(summed * B, stop * B)
        for i, (top, bottom, left, right) in enumerate(tiles):
            piece = product_nt(
                (m_hi[top:bottom, held], m_lo[top:bottom, held]),
                (w_hi[left:right, held], w_lo[left:right, held]),
            )
            sums[i] = piece if sums[i] is None else sums[i] + piece
        return stop

    for at in range(first, last):
        source = (before if at == first else work, first * B)
        rows, pending, part = factor_block(
            at, first, rows, pending, source, (work, first * B), (low_hi, low_lo),
            (tri_hi, tri_lo),
        )
        total = total + part
        goal = min(at, (at - first + 1) * count // (last - first))
        while done < goal:
            advance(done)
            done += 1
        if at + 2 == last or at + 1 == last:
            summed = accumulate(done)
    for k in range(done, count):
        advance(k)
    accumulate(count)
    for (top, bottom, left, right), block in zip(tiles, sums):
        for entry in range(left // B, right // B):
            base = sum((levels - i) * B for i in range(entry)) - entry * B
            part = block[:, entry * B - left : (entry + 1) * B - left]
            stop = min(bottom, levels * B)
            shared[base + top : base + stop, :] = part[: stop - top]
            if bottom > stop:
                tail[entry * extra : (entry + 1) * extra, :] = part[stop - top :]
    lane = lax.broadcasted_iota(jnp.int32, (SUB, B), 1)
    tail[levels * extra :, :] = jnp.where(lane == 0, total / points, 0.0)
    outgoing(shared, tail, send)


def outgoing(shared, tail, send):
    half = send.shape[0] - tail.shape[0]
    if half == shared.shape[0]:
        send[:half, :] = shared[...]
    else:
        start = pl.multiple_of((lax.axis_index("rep") % 2) * half, SUB)
        send[:half, :] = shared[pl.ds(start, half), :]
    send[half:, :] = tail[...]


def message_shapes(levels, extra):
    shared, half = halves(levels)
    tail = levels * extra + SUB
    return [jax.ShapeDtypeStruct((rows, B), F32) for rows in (shared, tail, half + tail)]


def forward(ranks, pieces, rhs, order, segments, parts, state):
    levels, _, points = pieces[0].shape
    extra = rhs.shape[0]
    rows = levels * B + extra
    inputs = [part for four in parts for part in four]
    shapes = (
        *message_shapes(levels, extra),
        jax.ShapeDtypeStruct((rows, points), BF16),
        jax.ShapeDtypeStruct((rows, points), BF16),
        jax.ShapeDtypeStruct((points, points), BF16),
        *segment_shapes(*segments[-1], points),
    )
    return pl.pallas_call(
        functools.partial(forward_kernel, levels, len(pieces), segments),
        out_shape=shapes,
        in_specs=[vmem()] * (8 + len(inputs) + len(pieces)),
        out_specs=(vmem(),) * len(shapes),
        scratch_shapes=[
            pltpu.VMEM(state[-1].shape, F32),
            pltpu.VMEM((rows, points), F32),
            pltpu.VMEM((rows, points), BF16),
            pltpu.VMEM((rows, points), BF16),
        ],
        **limit(16),
        name="forward",
    )(*state, ranks, *inputs, *pieces, rhs, order)


def backward_kernel(segments, *refs):
    parts = [refs[4 * i : 4 * i + 4] for i in range(len(segments))]
    w_hi, w_lo, v_hi, v_mid, v_last = refs[4 * len(segments) :]
    points = w_hi.shape[1]
    for (low_hi, low_lo, tri_hi, tri_lo), (first, last) in reversed(list(zip(parts, segments))):
        for k in reversed(range(first, last)):
            start, end = k * B, (k + 1) * B
            own = w_hi[:, start:end].astype(F32) + w_lo[:, start:end].astype(F32)
            if end < points:
                own = own - product_nn(
                    (v_hi[:, end:], v_mid[:, end:]),
                    below_of((low_hi, low_lo), first, k, end, points),
                )
            solved = product_nn(
                split(own), (tri_hi[k - first, B:, :], tri_lo[k - first, B:, :])
            )
            hi, mid, rest = thirds(solved)
            v_hi[:, start:end] = hi
            v_mid[:, start:end] = mid
            v_last[:, start:end] = rest


def backward(segments, parts, w_hi, w_lo):
    inputs = [part for four in parts for part in four]
    return pl.pallas_call(
        functools.partial(backward_kernel, segments),
        out_shape=(jax.ShapeDtypeStruct(w_hi.shape, BF16),) * 3,
        in_specs=[vmem()] * (2 + len(inputs)),
        out_specs=(vmem(),) * 3,
        **limit(10, 4 * 10**9),
        name="backward",
    )(*inputs, w_hi, w_lo)


def unorder_kernel(v_hi, v_mid, v_last, perm, out):
    sensors = perm[...]
    out[...] = dot_nt(v_hi[...], sensors) + (dot_nt(v_mid[...], sensors) + dot_nt(v_last[...], sensors))


def unorder(solved, perm):
    return pl.pallas_call(
        unorder_kernel,
        out_shape=jax.ShapeDtypeStruct(solved[0].shape, F32),
        in_specs=[vmem()] * 4,
        out_specs=vmem(),
        **limit(12, 4 * 10**9),
        name="unorder",
    )(*solved, perm)


def eliminate(depth, levels, extra, refs):
    shared, tail, received, *other, merged, below, corner = refs
    left = levels - depth
    whole, half = halves(left)
    if other:
        start = pl.multiple_of((lax.axis_index("rep") % 2) * half, SUB)
        across = pl.multiple_of(half - start, SUB)
        merged[pl.ds(start, half), :] = shared[pl.ds(start, half), :] + received[:half, :]
        merged[pl.ds(across, half), :] = shared[pl.ds(across, half), :] + other[0][...]
    else:
        merged[...] = shared[...] + received[:half, :]
    below[...] = tail[...] + received[half:, :]
    row = lax.broadcasted_iota(jnp.int32, (B, B), 0)
    column = lax.broadcasted_iota(jnp.int32, (B, B), 1)
    corner[...] = merged[:B, :] + jnp.where(row == column, 1.0, 0.0)
    tri, pivots = sweep(rows_from(corner))
    lane = lax.broadcasted_iota(jnp.int32, (SUB, B), 1)
    totals = below[left * extra :, :] + jnp.where(
        lane == depth + 1, log_sum(pivots) / B, 0.0
    )
    pieces = split(tri)
    panel = join([merged[B : left * B, :], below[:extra, :]], 0) if left > 1 else below[:extra, :]
    both = product_nt(split(panel), pieces)
    return pieces, both, totals


def merge_kernel(depth, levels, extra, *refs):
    inputs = refs[:4]
    next_shared, next_tail, send, w_out, tri_out = refs[4:9]
    scratch = refs[9:]
    merged, below = scratch[:2]
    pieces, both, totals = eliminate(depth, levels, extra, inputs + scratch)
    left = levels - depth - 1
    w_parts = split(both[:, :B])
    m_parts = split(both[:, B:])
    w_out[...] = both[:, :B]
    tri_out[...] = pieces[0][B:].astype(F32) + pieces[1][B:].astype(F32)
    at = 0
    for entry in range(left):
        top = entry * B
        rows = (left - entry) * B
        change = product_nt(
            tuple(part[top:] for part in m_parts),
            tuple(part[top : top + B] for part in w_parts),
        )
        base = (left + 1) * B + at
        next_shared[at : at + rows, :] = merged[base : base + rows, :] - change[:rows]
        next_tail[entry * extra : (entry + 1) * extra, :] = (
            below[(entry + 1) * extra : (entry + 2) * extra, :] - change[rows:]
        )
        at += rows
    next_tail[left * extra :, :] = totals
    outgoing(next_shared, next_tail, send)


def scratch_for(levels, extra):
    shared, tail, _ = message_shapes(levels, extra)
    return [
        pltpu.VMEM(shared.shape, F32),
        pltpu.VMEM(tail.shape, F32),
        pltpu.VMEM((B, B), F32),
    ]


def merge(depth, levels, extra, message):
    left = levels - depth
    return pl.pallas_call(
        functools.partial(merge_kernel, depth, levels, extra),
        out_shape=(
            *message_shapes(left - 1, extra),
            jax.ShapeDtypeStruct(((left - 1) * B + extra, B), F32),
            jax.ShapeDtypeStruct((B, B), F32),
        ),
        in_specs=[vmem()] * 4,
        out_specs=(vmem(),) * 5,
        scratch_shapes=scratch_for(left, extra),
        **limit(6),
        name="merge",
    )(*message)


def finish_kernel(levels, leaf_count, *refs):
    solved = refs[3]
    last = 4 + 2 * (levels - 1)
    saved = refs[4:last]
    out, means = refs[last : last + 2]
    extra = out.shape[0]
    depth = levels - 1
    pieces, both, totals = eliminate(depth, levels, extra, refs[:3] + refs[last + 2 :])
    coeffs = [None] * levels
    coeffs[depth] = split(
        product_nn(split(both[:, :B]), tuple(part[B:] for part in pieces))
    )
    for level in reversed(range(levels - 1)):
        w_ref, tri_ref = saved[2 * level], saved[2 * level + 1]
        inner = (levels - level - 1) * B
        known = tuple(
            join([coeffs[m][part] for m in range(level + 1, levels)], 1) for part in range(2)
        )
        target = w_ref[inner:, :] - product_nn(known, split(w_ref[:inner, :]))
        coeffs[level] = split(product_nn(split(target), split(tri_ref[...])))
    known = tuple(join([coeffs[m][part] for m in range(levels)], 1) for part in range(2))
    out[...] = solved[levels * B :, :] - product_nn(known, split(solved[: levels * B, :]))
    lane = lax.broadcasted_iota(jnp.int32, (SUB, B), 1)
    scale = jnp.zeros((SUB, B), F32)
    for entry in range(levels + 1):
        scale = jnp.where(lane == entry, 2.0**entry / leaf_count, scale)
    means[...] = (totals * scale)[:1, : levels + 1]


def finish(levels, leaf_count, extra, message, solved, saved):
    points = solved.shape[1]
    return pl.pallas_call(
        functools.partial(finish_kernel, levels, leaf_count),
        out_shape=(
            jax.ShapeDtypeStruct((extra, points), F32),
            jax.ShapeDtypeStruct((1, levels + 1), F32),
        ),
        in_specs=[vmem()] * (4 + len(saved)),
        out_specs=(vmem(),) * 2,
        scratch_shapes=scratch_for(1, extra),
        **limit(6),
        name="finish",
    )(*message, solved, *saved)


def swapped(value, axis, mask):
    pairs = [(source, source ^ mask) for source in range(lax.axis_size(axis))]
    return lax.ppermute(value, axis, pairs)


def exchange(message, depth, left, meanwhile=None):
    shared, tail, send = message
    received = swapped(send, "leaf", 2**depth)
    done = None
    if meanwhile is not None:
        received, done = lax.optimization_barrier((received, meanwhile()))
    if send.shape[0] == shared.shape[0] + tail.shape[0]:
        return (shared, tail, received), done
    other = swapped(received[: halves(left)[1]], "rep", 1)
    return (shared, tail, received, other), done


def shards(leaf_blocks, generators, rhs, order, ranks):
    levels = generators.shape[0]
    extra = rhs.shape[0]
    points = leaf_blocks.shape[1]
    count = points // B
    cuts = (0, 3 * count // 8, count // 2, count)
    segments = list(zip(cuts[:-1], cuts[1:]))
    size = lax.axis_size("rep")
    near = swapped(generators, "rep", 1)
    pieces = [generators, near]
    far = [swapped(generators, "rep", shift) for shift in range(2, size, 2)]
    *part, logs, corner, mult_hi, mult_lo, rest = head(*segments[0], leaf_blocks)
    parts = [part]
    far, logs = lax.optimization_barrier((far, logs))
    for arrived in far:
        pieces += [arrived, swapped(arrived, "rep", 1)]
    *part, logs, corner, mult_hi, mult_lo, rest = middle(
        *segments[1], points, part[:2], (logs, corner, mult_hi, mult_lo, rest)
    )
    parts.append(part)
    *message, w_hi, w_lo, perm, a, b, c, d = forward(
        ranks.T, pieces, rhs, order, segments, parts, (logs, corner, mult_hi, mult_lo, rest)
    )
    parts.append([a, b, c, d])
    saved, solved = [], None
    jobs = [lambda: backward(segments, parts, w_hi, w_lo), lambda: unorder(solved, perm)]
    for depth in range(levels - 1):
        arrived, done = exchange(message, depth, levels - depth, jobs.pop(0) if jobs else None)
        solved = solved if done is None else done
        *message, w_level, tri_level = merge(depth, levels, extra, arrived)
        saved += [w_level, tri_level]
    arrived, _ = exchange(message, levels - 1, 1)
    out, means = finish(levels, lax.axis_size("leaf"), extra, arrived, solved, saved)
    return (out, means.reshape(levels + 1))


def solution(mesh):
    placed = (
        P("leaf", None),
        P(None, "rep", "leaf"),
        P("rep", "leaf"),
        P("leaf", None),
        P(None, "leaf"),
    )
    return jax.shard_map(
        shards, mesh=mesh, in_specs=placed, out_specs=(P("rep", "leaf"), P()), check_vma=False
    )
```

```python
import functools

import jax
import jax.numpy as jnp
from jax import lax
from jax.experimental import pallas as pl
from jax.experimental.pallas import tpu as pltpu
from jax.sharding import PartitionSpec as P

F32 = jnp.float32
BF16 = jnp.bfloat16
B = 128
SUB = 8


def limit(mebibytes, flops=0):
    return dict(
        compiler_params=pltpu.CompilerParams(vmem_limit_bytes=mebibytes * 2**20),
        cost_estimate=pl.CostEstimate(flops=flops, bytes_accessed=2**20, transcendentals=0),
    )


def vmem():
    return pl.BlockSpec(memory_space=pltpu.VMEM)


def lanes_of(value, lane):
    index = jnp.full((SUB, B), lane, jnp.int32)
    return jnp.take_along_axis(value, index, axis=1, mode="promise_in_bounds")


def row_of(value, row):
    return jnp.broadcast_to(value[row : row + 1, :], (SUB, B))


def sweep(rows):
    lane = lax.broadcasted_iota(jnp.int32, (SUB, B), 1)
    sub = lax.broadcasted_iota(jnp.int32, (SUB, B), 0)
    count = B // SUB
    pivots = jnp.ones((SUB, B), F32)
    rows = list(rows)
    t, rt = [None] * count, [None] * count
    cols = [lanes_of(rows[0], l) for l in range(SUB)]
    for p in range(count):
        base = SUB * p
        inside = (lane >= base) & (lane < base + SUB)
        upto = lane < base + SUB
        panel = jnp.where(inside, jnp.where(lane - base == sub, 1.0, 0.0), rows[p])
        t[p] = jnp.where(upto, panel, 0.0)
        following = p + 1 < count
        ahead = None
        if following:
            first = [lanes_of(rows[p + 1], base + l) for l in range(SUB)]
            below = list(first)
            ahead = [lanes_of(rows[p + 1], base + SUB + l) for l in range(SUB)]
        for j in range(SUB):
            across = {l: row_of(cols[l], j) for l in range(j, SUB)}
            pivots = jnp.where(lane == base + j, across[j], pivots)
            inverse = pltpu.reciprocal(across[j], approx=True)
            scale = jnp.where(sub == j, 1.0 - inverse, cols[j] * inverse)
            for l in range(j + 1, SUB):
                cols[l] = cols[l] - scale * across[l]
            panel = panel - scale * row_of(panel, j)
            if following:
                factor = below[j] * inverse
                for l in range(SUB):
                    ahead[l] = ahead[l] - factor * row_of(below[j], l)
                for l in range(j + 1, SUB):
                    below[l] = below[l] - factor * across[l]
        rt[p] = jnp.where(upto, panel, 0.0)
        if following:
            spread = [row_of(panel, i) for i in range(SUB)]
        for q in range(p + 1, count):
            weight = first if q == p + 1 else [lanes_of(rows[q], base + l) for l in range(SUB)]
            even = jnp.where(inside, 0.0, rows[q]) - weight[0] * spread[0]
            odd = weight[1] * spread[1]
            for l in range(2, SUB, 2):
                even = even - weight[l] * spread[l]
                odd = odd + weight[l + 1] * spread[l + 1]
            rows[q] = even - odd
        cols = ahead
    return jnp.concatenate(t + rt, axis=0), pivots


def rows_from(ref):
    return [ref[SUB * p : SUB * (p + 1), :B] for p in range(B // SUB)]


def split(value):
    high = value.astype(BF16)
    return high, (value - high.astype(F32)).astype(BF16)


def dot_nt(left, right):
    return lax.dot_general(left, right, (((1,), (1,)), ((), ())), preferred_element_type=F32)


def dot_nn(left, right):
    return lax.dot_general(left, right, (((1,), (0,)), ((), ())), preferred_element_type=F32)


def join(parts, axis):
    return jnp.concatenate(parts, axis=axis)


def product_nt(left, right):
    lh, ll = left
    rh, rl = right
    return dot_nt(join([lh, lh, ll], 1), join([rh, rl, rh], 1))


def product_nn(left, right):
    lh, ll = left
    rh, rl = right
    return dot_nn(join([lh, lh, ll], 1), join([rh, rl, rh], 0))


def log_sum(pivots):
    return jnp.sum(jnp.log(pivots[:1]), axis=1, keepdims=True)


def eliminate_column(panel, corner, tri):
    both = product_nt(split(panel[:B]), tri)
    below, mult = split(both[:, :B]), split(both[:, B:])
    corner = corner - product_nt(mult, below)
    if panel.shape[0] > B:
        both = product_nt(split(panel[B:]), tri)
        below = tuple(join(pair, 0) for pair in zip(below, split(both[:, :B])))
        mult = tuple(join(pair, 0) for pair in zip(mult, split(both[:, B:])))
    return below, mult, [corner[SUB * p : SUB * (p + 1)] for p in range(B // SUB)]


def trail(source, target, mult, below):
    src, src_off = source
    dst, dst_off = target
    size = mult[0].shape[0]
    for col in range(0, size, B):
        change = product_nt(
            tuple(part[col:] for part in mult), tuple(part[col : col + B] for part in below)
        )
        fresh = src[src_off + col : src_off + size, src_off + col : src_off + col + B] - change
        dst[dst_off + col : dst_off + size, dst_off + col : dst_off + col + B] = fresh


def head_kernel(
    cut, blocks, low_hi, low_lo, tri_hi, tri_lo, logs, work, corner, sems
):
    points = work.shape[0]
    whole_copy = pltpu.make_async_copy(blocks, work, sems.at[0])
    first_copy = pltpu.make_async_copy(blocks.at[:B, :B], corner, sems.at[1])
    first_copy.start()
    whole_copy.start()
    first_copy.wait()
    tri, pivots = sweep(rows_from(corner))
    tri_hi[0], tri_lo[0] = split(tri)
    whole_copy.wait()

    def step(k, total):
        below, mult, rows = eliminate_column(
            work[B:, :B], work[B : 2 * B, B : 2 * B], (tri_hi[k], tri_lo[k])
        )
        low_hi[k], low_lo[k] = below
        tri, pivots = sweep(rows)
        tri_hi[k + 1], tri_lo[k + 1] = split(tri)
        trail((work, B), (work, 0), mult, below)
        return total + log_sum(pivots)

    total = lax.fori_loop(0, cut, step, log_sum(pivots))
    logs[...] = jnp.broadcast_to(total, logs.shape)


def head(cut, block):
    points = block.shape[1]
    low = jax.ShapeDtypeStruct((cut, points - B, B), BF16)
    tri = jax.ShapeDtypeStruct((cut + 1, 2 * B, B), BF16)
    return pl.pallas_call(
        functools.partial(head_kernel, cut),
        out_shape=(
            low,
            low,
            tri,
            tri,
            jax.ShapeDtypeStruct((SUB, B), F32),
            jax.ShapeDtypeStruct((points, points), F32),
        ),
        in_specs=[pl.BlockSpec(memory_space=pltpu.HBM)],
        out_specs=(vmem(),) * 6,
        scratch_shapes=[pltpu.VMEM((B, B), F32), pltpu.SemaphoreType.DMA((2,))],
        **limit(10),
        name="head",
    )(pltpu.with_memory_space_constraint(block, pltpu.HBM))


def permutation(order_ref, points):
    sensor = lax.broadcasted_iota(jnp.int32, (points, points), 0)
    return jnp.where(sensor == order_ref[...], 1.0, 0.0).astype(BF16)


def thirds(value):
    high = value.astype(BF16)
    rest = value - high.astype(F32)
    mid = rest.astype(BF16)
    return high, mid, (rest - mid.astype(F32)).astype(BF16)


def column_rows(levels, extra, entry):
    return (levels - entry) * B + extra


def halves(levels):
    shared = sum((levels - entry) * B for entry in range(levels))
    return shared, shared // 2 if levels > 1 else shared


def gram_tiles(levels, extra):
    bottom = levels * B + extra
    tiles = []
    for entry in range(0, levels, 2):
        left, mid, right = entry * B, (entry + 1) * B, (entry + 2) * B
        if entry + 1 < levels:
            tiles += [(left, mid, left, mid), (mid, bottom, left, right)]
        else:
            tiles.append((left, bottom, left, mid))
    return tiles


def prepare_kernel(rhs, order, perm, moved):
    extra, points = rhs.shape
    perm[...] = permutation(order, points)
    parts = dot_nn(join(thirds(rhs[...]), 0), perm[...])
    moved[...] = parts[:extra] + (parts[extra : 2 * extra] + parts[2 * extra :])


def prepare(rhs, order):
    points = rhs.shape[1]
    return pl.pallas_call(
        prepare_kernel,
        out_shape=(
            jax.ShapeDtypeStruct((points, points), BF16),
            jax.ShapeDtypeStruct(rhs.shape, F32),
        ),
        in_specs=[vmem()] * 2,
        out_specs=(vmem(),) * 2,
        **limit(8, 10**9),
        name="prepare",
    )(rhs, order)


def forward_kernel(levels, size, *refs):
    head_hi, head_lo, first_hi, first_lo, logs, before, ranks = refs[:7]
    pieces = refs[7 : 7 + size]
    moved, shared, tail, send, w_hi, w_lo, low_hi, low_lo, last_hi, last_lo = refs[
        7 + size : 17 + size
    ]
    work, values, m_hi, m_lo = refs[17 + size :]
    extra, points = moved.shape
    count = points // B
    cut = head_hi.shape[0]
    quarter = pieces[0].shape[1]
    own = lax.axis_index("rep")
    for level in range(levels):
        limit_here = ranks[:, level : level + 1]
        for shift in range(size):
            first = (own ^ shift) * quarter
            row = lax.broadcasted_iota(jnp.int32, (quarter, points), 0) + first
            at = pl.multiple_of(level * B + first, SUB)
            values[pl.ds(at, quarter), :] = jnp.where(
                row < limit_here, pieces[shift][level], 0.0
            )
    values[levels * B :, :] = moved[...]

    def tri_of(k):
        if k <= cut:
            return first_hi[k], first_lo[k]
        return last_hi[k - cut - 1], last_lo[k - cut - 1]

    def low_of(k, left, right):
        parts = []
        for old, new in ((head_hi, low_hi), (head_lo, low_lo)):
            blocks = [old[j, (k - j - 1) * B : (k - j) * B, :] for j in range(left, min(right, cut))]
            start = max(left, cut)
            if start < right:
                rows = slice((k - cut - 1) * B, (k - cut) * B)
                blocks.append(new[rows, (start - cut) * B : (right - cut) * B])
            parts.append(join(blocks, 1))
        return tuple(parts)

    def advance(k):
        start, end = k * B, (k + 1) * B
        here = values[:, start:end]
        for left, right in ((0, k - 1), (max(k - 1, 0), k)):
            if left < right:
                held = slice(left * B, right * B)
                here = here - product_nt((m_hi[:, held], m_lo[:, held]), low_of(k, left, right))
        both = product_nt(split(here), tri_of(k))
        w_hi[:, start:end], w_lo[:, start:end] = split(both[:, :B])
        m_hi[:, start:end], m_lo[:, start:end] = split(both[:, B:])

    total = logs[:1, :1]
    tiles = gram_tiles(levels, extra)
    sums = [None] * len(tiles)
    done, summed = 0, 0

    def accumulate(stop):
        held = slice(summed * B, stop * B)
        for i, (top, bottom, left, right) in enumerate(tiles):
            piece = product_nt(
                (m_hi[top:bottom, held], m_lo[top:bottom, held]),
                (w_hi[left:right, held], w_lo[left:right, held]),
            )
            sums[i] = piece if sums[i] is None else sums[i] + piece
        return stop

    for at in range(cut, count - 1):
        src = before if at == cut else work
        base = (at - cut) * B
        size_here = points - at * B
        below, mult, rows = eliminate_column(
            src[base + B : base + size_here, base : base + B],
            src[base + B : base + 2 * B, base + B : base + 2 * B],
            tri_of(at),
        )
        low_hi[base:, base : base + B], low_lo[base:, base : base + B] = below
        tri, pivots = sweep(rows)
        last_hi[at - cut], last_lo[at - cut] = split(tri)
        total = total + log_sum(pivots)
        trail((src, base + B), (work, base + B), mult, below)
        goal = min(at + 1, (at - cut + 1) * count // (count - 1 - cut))
        while done < goal:
            advance(done)
            done += 1
        if at + 3 >= count:
            summed = accumulate(done)
    for k in range(done, count):
        advance(k)
    accumulate(count)
    for (top, bottom, left, right), block in zip(tiles, sums):
        for entry in range(left // B, right // B):
            base = sum((levels - i) * B for i in range(entry)) - entry * B
            part = block[:, entry * B - left : (entry + 1) * B - left]
            stop = min(bottom, levels * B)
            shared[base + top : base + stop, :] = part[: stop - top]
            if bottom > stop:
                tail[entry * extra : (entry + 1) * extra, :] = part[stop - top :]
    lane = lax.broadcasted_iota(jnp.int32, (SUB, B), 1)
    tail[levels * extra :, :] = jnp.where(lane == 0, total / points, 0.0)
    outgoing(shared, tail, send)


def outgoing(shared, tail, send):
    half = send.shape[0] - tail.shape[0]
    if half == shared.shape[0]:
        send[:half, :] = shared[...]
    else:
        start = pl.multiple_of((lax.axis_index("rep") % 2) * half, SUB)
        send[:half, :] = shared[pl.ds(start, half), :]
    send[half:, :] = tail[...]


def message_shapes(levels, extra):
    shared, half = halves(levels)
    tail = levels * extra + SUB
    return [jax.ShapeDtypeStruct((rows, B), F32) for rows in (shared, tail, half + tail)]


def forward(ranks, pieces, moved, factors):
    levels, _, points = pieces[0].shape
    extra = moved.shape[0]
    rows = levels * B + extra
    count = points // B
    cut = factors[0].shape[0]
    left = (count - 1 - cut) * B
    low = jax.ShapeDtypeStruct((left, left), BF16)
    tri = jax.ShapeDtypeStruct((count - 1 - cut, 2 * B, B), BF16)
    half = jax.ShapeDtypeStruct((rows, points), BF16)
    return pl.pallas_call(
        functools.partial(forward_kernel, levels, len(pieces)),
        out_shape=(*message_shapes(levels, extra), half, half, low, low, tri, tri),
        in_specs=[vmem()] * (8 + len(pieces)),
        out_specs=(vmem(),) * 9,
        scratch_shapes=[
            pltpu.VMEM((left + B, left + B), F32),
            pltpu.VMEM((rows, points), F32),
            pltpu.VMEM((rows, points), BF16),
            pltpu.VMEM((rows, points), BF16),
        ],
        **limit(16),
        name="forward",
    )(*factors, ranks, *pieces, moved)


def reduce_rows(w_panel, tri, w_hi, w_lo):
    coeffs = split(product_nn(split(w_panel[...]), split(tri[...])))
    rest = w_hi[B:, :].astype(F32) + w_lo[B:, :].astype(F32)
    return split(rest - product_nn(coeffs, (w_hi[:B, :], w_lo[:B, :])))


def reduce_kernel(w_panel, tri, w_hi, w_lo, out_hi, out_lo):
    out_hi[...], out_lo[...] = reduce_rows(w_panel, tri, w_hi, w_lo)


def reduce(w_panel, tri, w_hi, w_lo):
    shape = jax.ShapeDtypeStruct((w_hi.shape[0] - B, w_hi.shape[1]), BF16)
    return pl.pallas_call(
        reduce_kernel,
        out_shape=(shape, shape),
        in_specs=[vmem()] * 4,
        out_specs=(vmem(),) * 2,
        **limit(8, 4 * 10**9),
        name="reduce",
    )(w_panel, tri, w_hi, w_lo)


def solve_kernel(
    head_hi, head_lo, first_hi, first_lo, low_hi, low_lo, last_hi, last_lo, perm,
    w_hi, w_lo, out, v_hi, v_mid, v_last,
):
    points = w_hi.shape[1]
    count = points // B
    cut = head_hi.shape[0]
    for k in reversed(range(count)):
        start, end = k * B, (k + 1) * B
        here = w_hi[:, start:end].astype(F32) + w_lo[:, start:end].astype(F32)
        for left, right in ((end + B, points), (end, min(end + B, points))):
            if left >= right:
                continue
            if k < cut:
                rows = slice(left - end, right - end)
                below = head_hi[k, rows, :], head_lo[k, rows, :]
            else:
                rows = slice(left - (cut + 1) * B, right - (cut + 1) * B)
                columns = slice((k - cut) * B, (k - cut + 1) * B)
                below = low_hi[rows, columns], low_lo[rows, columns]
            here = here - product_nn((v_hi[:, left:right], v_mid[:, left:right]), below)
        if k <= cut:
            tri = first_hi[k, B:, :], first_lo[k, B:, :]
        else:
            tri = last_hi[k - cut - 1, B:, :], last_lo[k - cut - 1, B:, :]
        parts = thirds(product_nn(split(here), tri))
        v_hi[:, start:end], v_mid[:, start:end], v_last[:, start:end] = parts
    sensors = perm[...]
    out[...] = dot_nt(v_hi[...], sensors) + (
        dot_nt(v_mid[...], sensors) + dot_nt(v_last[...], sensors)
    )


def solve(factors, perm, w_hi, w_lo):
    return pl.pallas_call(
        solve_kernel,
        out_shape=jax.ShapeDtypeStruct(w_hi.shape, F32),
        in_specs=[vmem()] * (3 + len(factors)),
        out_specs=vmem(),
        scratch_shapes=[pltpu.VMEM(w_hi.shape, BF16)] * 3,
        **limit(10, 4 * 10**9),
        name="solve",
    )(*factors, perm, w_hi, w_lo)


def eliminate(depth, levels, extra, refs):
    shared, tail, received, *other, merged, below, corner = refs
    left = levels - depth
    whole, half = halves(left)
    if other:
        start = pl.multiple_of((lax.axis_index("rep") % 2) * half, SUB)
        across = pl.multiple_of(half - start, SUB)
        merged[pl.ds(start, half), :] = shared[pl.ds(start, half), :] + received[:half, :]
        merged[pl.ds(across, half), :] = shared[pl.ds(across, half), :] + other[0][...]
    else:
        merged[...] = shared[...] + received[:half, :]
    below[...] = tail[...] + received[half:, :]
    row = lax.broadcasted_iota(jnp.int32, (B, B), 0)
    column = lax.broadcasted_iota(jnp.int32, (B, B), 1)
    corner[...] = merged[:B, :] + jnp.where(row == column, 1.0, 0.0)
    tri, pivots = sweep(rows_from(corner))
    lane = lax.broadcasted_iota(jnp.int32, (SUB, B), 1)
    totals = below[left * extra :, :] + jnp.where(
        lane == depth + 1, log_sum(pivots) / B, 0.0
    )
    pieces = split(tri)
    panel = join([merged[B : left * B, :], below[:extra, :]], 0) if left > 1 else below[:extra, :]
    both = product_nt(split(panel), pieces)
    return pieces, both, totals


def merge_kernel(depth, levels, extra, *refs):
    inputs = refs[:4]
    next_shared, next_tail, send, w_out, tri_out = refs[4:9]
    scratch = refs[9:]
    merged, below = scratch[:2]
    pieces, both, totals = eliminate(depth, levels, extra, inputs + scratch)
    left = levels - depth - 1
    w_parts = split(both[:, :B])
    m_parts = split(both[:, B:])
    w_out[...] = both[:, :B]
    tri_out[...] = pieces[0][B:].astype(F32) + pieces[1][B:].astype(F32)
    at = 0
    for entry in range(left):
        top = entry * B
        rows = (left - entry) * B
        change = product_nt(
            tuple(part[top:] for part in m_parts),
            tuple(part[top : top + B] for part in w_parts),
        )
        base = (left + 1) * B + at
        next_shared[at : at + rows, :] = merged[base : base + rows, :] - change[:rows]
        next_tail[entry * extra : (entry + 1) * extra, :] = (
            below[(entry + 1) * extra : (entry + 2) * extra, :] - change[rows:]
        )
        at += rows
    next_tail[left * extra :, :] = totals
    outgoing(next_shared, next_tail, send)


def scratch_for(levels, extra):
    shared, tail, _ = message_shapes(levels, extra)
    return [
        pltpu.VMEM(shared.shape, F32),
        pltpu.VMEM(tail.shape, F32),
        pltpu.VMEM((B, B), F32),
    ]


def merge(depth, levels, extra, message):
    left = levels - depth
    return pl.pallas_call(
        functools.partial(merge_kernel, depth, levels, extra),
        out_shape=(
            *message_shapes(left - 1, extra),
            jax.ShapeDtypeStruct(((left - 1) * B + extra, B), F32),
            jax.ShapeDtypeStruct((B, B), F32),
        ),
        in_specs=[vmem()] * 4,
        out_specs=(vmem(),) * 5,
        scratch_shapes=scratch_for(left, extra),
        **limit(6),
        name="merge",
    )(*message)


def finish_kernel(levels, leaf_count, *refs):
    solved, out, means = refs[3:6]
    extra = out.shape[0]
    pieces, both, totals = eliminate(levels - 1, levels, extra, refs[:3] + refs[6:])
    coeffs = split(product_nn(split(both[:, :B]), tuple(part[B:] for part in pieces)))
    out[...] = solved[B:, :] - product_nn(coeffs, split(solved[:B, :]))
    lane = lax.broadcasted_iota(jnp.int32, (SUB, B), 1)
    scale = jnp.zeros((SUB, B), F32)
    for entry in range(levels + 1):
        scale = jnp.where(lane == entry, 2.0**entry / leaf_count, scale)
    means[...] = (totals * scale)[:1, : levels + 1]


def finish(levels, leaf_count, extra, message, solved):
    return pl.pallas_call(
        functools.partial(finish_kernel, levels, leaf_count),
        out_shape=(
            jax.ShapeDtypeStruct((extra, solved.shape[1]), F32),
            jax.ShapeDtypeStruct((1, levels + 1), F32),
        ),
        in_specs=[vmem()] * 4,
        out_specs=(vmem(),) * 2,
        scratch_shapes=scratch_for(1, extra),
        **limit(6),
        name="finish",
    )(*message, solved)


def swapped(value, axis, mask):
    pairs = [(source, source ^ mask) for source in range(lax.axis_size(axis))]
    return lax.ppermute(value, axis, pairs)


def exchange(message, depth, left, meanwhile=None):
    shared, tail, send = message
    received = swapped(send, "leaf", 2**depth)
    done = None
    if meanwhile is not None:
        received, done = lax.optimization_barrier((received, meanwhile()))
    if send.shape[0] == shared.shape[0] + tail.shape[0]:
        return (shared, tail, received), done
    other = swapped(received[: halves(left)[1]], "rep", 1)
    return (shared, tail, received, other), done


def shards(leaf_blocks, generators, rhs, order, ranks):
    levels = generators.shape[0]
    extra = rhs.shape[0]
    cut = leaf_blocks.shape[1] // B // 2 - 1
    pieces = [generators, swapped(generators, "rep", 1)]
    far = [swapped(generators, "rep", mask) for mask in range(2, lax.axis_size("rep"), 2)]
    *factors, logs, rest = head(cut, leaf_blocks)
    far, logs = lax.optimization_barrier((far, logs))
    for arrived in far:
        pieces += [arrived, swapped(arrived, "rep", 1)]
    perm, moved = prepare(rhs, order)
    *message, w_hi, w_lo, a, b, c, d = forward(
        ranks.T, pieces, moved, (*factors, logs, rest)
    )
    factors += [a, b, c, d]
    halves_of = (w_hi, w_lo)
    level = None
    for depth in range(levels):

        def meanwhile():
            rows = halves_of if level is None else reduce(*level, *halves_of)
            return solve(factors, perm, *rows) if depth + 1 == levels else rows

        arrived, halves_of = exchange(message, depth, levels - depth, meanwhile)
        if depth + 1 < levels:
            *message, w_level, tri_level = merge(depth, levels, extra, arrived)
            level = (w_level, tri_level)
    out, means = finish(levels, lax.axis_size("leaf"), extra, arrived, halves_of)
    return (out, means.reshape(levels + 1))


def solution(mesh):
    placed = (
        P("leaf", None),
        P(None, "rep", "leaf"),
        P("rep", "leaf"),
        P("leaf", None),
        P(None, "leaf"),
    )
    return jax.shard_map(
        shards, mesh=mesh, in_specs=placed, out_specs=(P("rep", "leaf"), P()), check_vma=False
    )
```

```python
import functools

import jax
import jax.numpy as jnp
from jax import lax
from jax.experimental import pallas as pl
from jax.experimental.pallas import tpu as pltpu
from jax.sharding import PartitionSpec as P

F32 = jnp.float32
BF16 = jnp.bfloat16
B = 128
SUB = 8


def limit(mebibytes, flops=0):
    return dict(
        compiler_params=pltpu.CompilerParams(vmem_limit_bytes=mebibytes * 2**20),
        cost_estimate=pl.CostEstimate(flops=flops, bytes_accessed=2**20, transcendentals=0),
    )


def vmem():
    return pl.BlockSpec(memory_space=pltpu.VMEM)


def lanes_of(value, lane):
    index = jnp.full((SUB, B), lane, jnp.int32)
    return jnp.take_along_axis(value, index, axis=1, mode="promise_in_bounds")


def row_of(value, row):
    return jnp.broadcast_to(value[row : row + 1, :], (SUB, B))


def sweep(rows, spare):
    lane = lax.broadcasted_iota(jnp.int32, (SUB, B), 1)
    sub = lax.broadcasted_iota(jnp.int32, (SUB, B), 0)
    count = B // SUB
    pivots = jnp.ones((SUB, B), F32)
    rows = list(rows)
    t, rt = [None] * count, [None] * count
    cols = [lanes_of(rows[0], l) for l in range(SUB)]

    def update(group, base, inside, spread):
        weights = [[] for _ in group]
        for l in range(SUB):
            for weight, q in zip(weights, group):
                weight.append(lanes_of(rows[q], base + l))
        for weight, q in zip(weights, group):
            apply(q, inside, spread, weight)

    def apply(q, inside, spread, weight):
        even = jnp.where(inside, 0.0, rows[q]) - weight[0] * spread[0]
        odd = weight[1] * spread[1]
        for l in range(2, SUB, 2):
            even = even - weight[l] * spread[l]
            odd = odd + weight[l + 1] * spread[l + 1]
        rows[q] = even - odd

    for p in range(count):
        base = SUB * p
        inside = (lane >= base) & (lane < base + SUB)
        upto = lane < base + SUB
        panel = jnp.where(inside, jnp.where(lane - base == sub, 1.0, 0.0), rows[p])
        t[p] = jnp.where(upto, panel, 0.0)
        following = p + 1 < count
        ahead = None
        if following:
            first = [lanes_of(rows[p + 1], base + l) for l in range(SUB)]
            below = list(first)
            ahead = [lanes_of(rows[p + 1], base + SUB + l) for l in range(SUB)]
        for j in range(SUB):
            across = {l: row_of(cols[l], j) for l in range(j, SUB)}
            pivots = jnp.where(lane == base + j, across[j], pivots)
            inverse = pltpu.reciprocal(across[j], approx=True)
            scale = jnp.where(sub == j, 1.0 - inverse, cols[j] * inverse)
            for l in range(j + 1, SUB):
                cols[l] = cols[l] - scale * across[l]
            panel = panel - scale * row_of(panel, j)
            if following:
                slot = (p % 2) * SUB + j
                spare[slot, :SUB, :] = below[j]
                factor = below[j] * inverse
                for l in range(SUB):
                    ahead[l] = ahead[l] - factor * spare[slot, pl.ds(l, SUB, stride=0), :]
                for l in range(j + 1, SUB):
                    below[l] = below[l] - factor * across[l]
        rt[p] = jnp.where(upto, panel, 0.0)
        if following:
            spread = [row_of(panel, i) for i in range(SUB)]
            apply(p + 1, inside, spread, first)
            update(list(range(p + 2, min(p + 3, count))), base, inside, spread)
            for q in range(p + 3, count, 3):
                update(list(range(q, min(q + 3, count))), base, inside, spread)
        cols = ahead
    return jnp.concatenate(t + rt, axis=0), pivots


def spare_rows():
    return pltpu.VMEM((2 * SUB, 2 * SUB, B), F32)


def rows_from(ref):
    return [ref[SUB * p : SUB * (p + 1), :B] for p in range(B // SUB)]


def split(value):
    high = value.astype(BF16)
    return high, (value - high.astype(F32)).astype(BF16)


def dot_nt(left, right):
    return lax.dot_general(left, right, (((1,), (1,)), ((), ())), preferred_element_type=F32)


def dot_nn(left, right):
    return lax.dot_general(left, right, (((1,), (0,)), ((), ())), preferred_element_type=F32)


def join(parts, axis):
    return jnp.concatenate(parts, axis=axis)


def product_nt(left, right):
    lh, ll = left
    rh, rl = right
    return dot_nt(join([lh, lh, ll], 1), join([rh, rl, rh], 1))


def product_nn(left, right):
    lh, ll = left
    rh, rl = right
    return dot_nn(join([lh, lh, ll], 1), join([rh, rl, rh], 0))


def log_sum(pivots):
    return jnp.sum(jnp.log(pivots[:1]), axis=1, keepdims=True)


def eliminate_column(panel, corner, tri):
    both = product_nt(split(panel[:B]), tri)
    below, mult = split(both[:, :B]), split(both[:, B:])
    corner = corner - product_nt(mult, below)
    if panel.shape[0] > B:
        both = product_nt(split(panel[B:]), tri)
        below = tuple(join(pair, 0) for pair in zip(below, split(both[:, :B])))
        mult = tuple(join(pair, 0) for pair in zip(mult, split(both[:, B:])))
    return below, mult, [corner[SUB * p : SUB * (p + 1)] for p in range(B // SUB)]


def trail(source, target, mult, below):
    src, src_off = source
    dst, dst_off = target
    size = mult[0].shape[0]
    for col in range(0, size, B):
        change = product_nt(
            tuple(part[col:] for part in mult), tuple(part[col : col + B] for part in below)
        )
        fresh = src[src_off + col : src_off + size, src_off + col : src_off + col + B] - change
        dst[dst_off + col : dst_off + size, dst_off + col : dst_off + col + B] = fresh


def head_kernel(
    cut, blocks, low_hi, low_lo, tri_hi, tri_lo, logs, work, corner, spare, sems
):
    points = work.shape[0]
    whole_copy = pltpu.make_async_copy(blocks, work, sems.at[0])
    first_copy = pltpu.make_async_copy(blocks.at[:B, :B], corner, sems.at[1])
    first_copy.start()
    whole_copy.start()
    first_copy.wait()
    tri, pivots = sweep(rows_from(corner), spare)
    tri_hi[0], tri_lo[0] = split(tri)
    whole_copy.wait()

    def step(k, total):
        below, mult, rows = eliminate_column(
            work[B:, :B], work[B : 2 * B, B : 2 * B], (tri_hi[k], tri_lo[k])
        )
        low_hi[k], low_lo[k] = below
        tri, pivots = sweep(rows, spare)
        tri_hi[k + 1], tri_lo[k + 1] = split(tri)
        trail((work, B), (work, 0), mult, below)
        return total + log_sum(pivots)

    total = lax.fori_loop(0, cut, step, log_sum(pivots))
    logs[...] = jnp.broadcast_to(total, logs.shape)


def head(cut, block):
    points = block.shape[1]
    low = jax.ShapeDtypeStruct((cut, points - B, B), BF16)
    tri = jax.ShapeDtypeStruct((cut + 1, 2 * B, B), BF16)
    return pl.pallas_call(
        functools.partial(head_kernel, cut),
        out_shape=(
            low,
            low,
            tri,
            tri,
            jax.ShapeDtypeStruct((SUB, B), F32),
            jax.ShapeDtypeStruct((points, points), F32),
        ),
        in_specs=[pl.BlockSpec(memory_space=pltpu.HBM)],
        out_specs=(vmem(),) * 6,
        scratch_shapes=[
            pltpu.VMEM((B, B), F32),
            spare_rows(),
            pltpu.SemaphoreType.DMA((2,)),
        ],
        **limit(10),
        name="head",
    )(pltpu.with_memory_space_constraint(block, pltpu.HBM))


def permutation(order_ref, points):
    sensor = lax.broadcasted_iota(jnp.int32, (points, points), 0)
    return jnp.where(sensor == order_ref[...], 1.0, 0.0).astype(BF16)


def thirds(value):
    high = value.astype(BF16)
    rest = value - high.astype(F32)
    mid = rest.astype(BF16)
    return high, mid, (rest - mid.astype(F32)).astype(BF16)


def column_rows(levels, extra, entry):
    return (levels - entry) * B + extra


def halves(levels):
    rest = sum((levels - entry) * B for entry in range(levels)) - B
    return B, rest, B // 2 if levels > 1 else B, rest // 2


def half_of(size):
    start = pl.multiple_of((lax.axis_index("rep") % 2) * size, SUB)
    return start, pl.multiple_of(size - start, SUB)


def gram_tiles(levels, extra):
    bottom = levels * B + extra
    tiles = []
    for entry in range(0, levels, 2):
        left, mid, right = entry * B, (entry + 1) * B, (entry + 2) * B
        if entry + 1 < levels:
            tiles += [(left, mid, left, mid), (mid, bottom, left, right)]
        else:
            tiles.append((left, bottom, left, mid))
    return tiles


def prepare_kernel(rhs, order, perm, moved):
    extra, points = rhs.shape
    perm[...] = permutation(order, points)
    parts = dot_nn(join(thirds(rhs[...]), 0), perm[...])
    moved[...] = parts[:extra] + (parts[extra : 2 * extra] + parts[2 * extra :])


def prepare(rhs, order):
    points = rhs.shape[1]
    return pl.pallas_call(
        prepare_kernel,
        out_shape=(
            jax.ShapeDtypeStruct((points, points), BF16),
            jax.ShapeDtypeStruct(rhs.shape, F32),
        ),
        in_specs=[vmem()] * 2,
        out_specs=(vmem(),) * 2,
        **limit(8, 10**9),
        name="prepare",
    )(rhs, order)


def forward_kernel(levels, size, *refs):
    head_hi, head_lo, first_hi, first_lo, logs, before, ranks = refs[:7]
    pieces = refs[7 : 7 + size]
    moved = refs[7 + size]
    *sends, w_hi, w_lo, low_hi, low_lo, last_hi, last_lo = refs[10 + size : -5]
    shared, tail = refs[8 + size : 10 + size]
    work, values, m_hi, m_lo, spare = refs[-5:]
    extra, points = moved.shape
    count = points // B
    cut = head_hi.shape[0]
    quarter = pieces[0].shape[1]
    own = lax.axis_index("rep")
    for level in range(levels):
        limit_here = ranks[:, level : level + 1]
        for shift in range(size):
            first = (own ^ shift) * quarter
            row = lax.broadcasted_iota(jnp.int32, (quarter, points), 0) + first
            at = pl.multiple_of(level * B + first, SUB)
            values[pl.ds(at, quarter), :] = jnp.where(
                row < limit_here, pieces[shift][level], 0.0
            )
    values[levels * B :, :] = moved[...]

    def tri_of(k):
        if k <= cut:
            return first_hi[k], first_lo[k]
        return last_hi[k - cut - 1], last_lo[k - cut - 1]

    def low_of(k, left, right):
        parts = []
        for old, new in ((head_hi, low_hi), (head_lo, low_lo)):
            blocks = [old[j, (k - j - 1) * B : (k - j) * B, :] for j in range(left, min(right, cut))]
            start = max(left, cut)
            if start < right:
                rows = slice((k - cut - 1) * B, (k - cut) * B)
                blocks.append(new[rows, (start - cut) * B : (right - cut) * B])
            parts.append(join(blocks, 1))
        return tuple(parts)

    def advance(k):
        start, end = k * B, (k + 1) * B
        here = values[:, start:end]
        for left, right in ((0, k - 1), (max(k - 1, 0), k)):
            if left < right:
                held = slice(left * B, right * B)
                here = here - product_nt((m_hi[:, held], m_lo[:, held]), low_of(k, left, right))
        both = product_nt(split(here), tri_of(k))
        w_hi[:, start:end], w_lo[:, start:end] = split(both[:, :B])
        m_hi[:, start:end], m_lo[:, start:end] = split(both[:, B:])

    total = logs[:1, :1]
    tiles = gram_tiles(levels, extra)
    sums = [None] * len(tiles)
    done, summed = 0, 0

    def accumulate(stop):
        held = slice(summed * B, stop * B)
        for i, (top, bottom, left, right) in enumerate(tiles):
            piece = product_nt(
                (m_hi[top:bottom, held], m_lo[top:bottom, held]),
                (w_hi[left:right, held], w_lo[left:right, held]),
            )
            sums[i] = piece if sums[i] is None else sums[i] + piece
        return stop

    for at in range(cut, count - 1):
        src = before if at == cut else work
        base = (at - cut) * B
        size_here = points - at * B
        below, mult, rows = eliminate_column(
            src[base + B : base + size_here, base : base + B],
            src[base + B : base + 2 * B, base + B : base + 2 * B],
            tri_of(at),
        )
        low_hi[base:, base : base + B], low_lo[base:, base : base + B] = below
        tri, pivots = sweep(rows, spare)
        last_hi[at - cut], last_lo[at - cut] = split(tri)
        total = total + log_sum(pivots)
        trail((src, base + B), (work, base + B), mult, below)
        goal = min(at + 1, (at - cut + 1) * count // (count - 1 - cut))
        while done < goal:
            advance(done)
            done += 1
        if at + 3 >= count:
            summed = accumulate(done)
    for k in range(done, count):
        advance(k)
    accumulate(count)
    for (top, bottom, left, right), block in zip(tiles, sums):
        for entry in range(left // B, right // B):
            base = sum((levels - i) * B for i in range(entry)) - entry * B
            part = block[:, entry * B - left : (entry + 1) * B - left]
            stop = min(bottom, levels * B)
            shared[base + top : base + stop, :] = part[: stop - top]
            if bottom > stop:
                tail[entry * extra : (entry + 1) * extra, :] = part[stop - top :]
    lane = lax.broadcasted_iota(jnp.int32, (SUB, B), 1)
    tail[levels * extra :, :] = jnp.where(lane == 0, total / points, 0.0)
    outgoing(shared, tail, *sends)


def outgoing(shared, tail, *sends):
    if len(sends) == 1:
        sends[0][:B, :] = shared[...]
        sends[0][B:, :] = tail[...]
        return
    corner, others = sends
    corner[...] = shared[pl.ds(half_of(B // 2)[0], B // 2), :]
    half = others.shape[0] - tail.shape[0]
    others[:half, :] = shared[pl.ds(B + half_of(half)[0], half), :]
    others[half:, :] = tail[...]


def message_shapes(levels, extra):
    first, rest, half_first, half_rest = halves(levels)
    tail = levels * extra + SUB
    if levels > 1:
        sends = (half_first, half_rest + tail)
    else:
        sends = (first + tail,)
    return [jax.ShapeDtypeStruct((rows, B), F32) for rows in (first + rest, tail, *sends)]


def forward(ranks, pieces, moved, factors):
    levels, _, points = pieces[0].shape
    extra = moved.shape[0]
    rows = levels * B + extra
    count = points // B
    cut = factors[0].shape[0]
    left = (count - 1 - cut) * B
    low = jax.ShapeDtypeStruct((left, left), BF16)
    tri = jax.ShapeDtypeStruct((count - 1 - cut, 2 * B, B), BF16)
    half = jax.ShapeDtypeStruct((rows, points), BF16)
    return pl.pallas_call(
        functools.partial(forward_kernel, levels, len(pieces)),
        out_shape=(*message_shapes(levels, extra), half, half, low, low, tri, tri),
        in_specs=[vmem()] * (8 + len(pieces)),
        out_specs=(vmem(),) * (6 + len(message_shapes(levels, extra))),
        scratch_shapes=[
            pltpu.VMEM((left + B, left + B), F32),
            pltpu.VMEM((rows, points), F32),
            pltpu.VMEM((rows, points), BF16),
            pltpu.VMEM((rows, points), BF16),
            spare_rows(),
        ],
        **limit(16),
        name="forward",
    )(*factors, ranks, *pieces, moved)


def reduce_rows(w_panel, tri, w_hi, w_lo):
    coeffs = split(product_nn(split(w_panel[...]), split(tri[...])))
    rest = w_hi[B:, :].astype(F32) + w_lo[B:, :].astype(F32)
    return split(rest - product_nn(coeffs, (w_hi[:B, :], w_lo[:B, :])))


def reduce_kernel(w_panel, tri, w_hi, w_lo, out_hi, out_lo):
    out_hi[...], out_lo[...] = reduce_rows(w_panel, tri, w_hi, w_lo)


def reduce(w_panel, tri, w_hi, w_lo):
    shape = jax.ShapeDtypeStruct((w_hi.shape[0] - B, w_hi.shape[1]), BF16)
    return pl.pallas_call(
        reduce_kernel,
        out_shape=(shape, shape),
        in_specs=[vmem()] * 4,
        out_specs=(vmem(),) * 2,
        **limit(8, 4 * 10**9),
        name="reduce",
    )(w_panel, tri, w_hi, w_lo)


def solve_kernel(
    head_hi, head_lo, first_hi, first_lo, low_hi, low_lo, last_hi, last_lo, perm,
    w_hi, w_lo, out, v_hi, v_mid, v_last,
):
    points = w_hi.shape[1]
    count = points // B
    cut = head_hi.shape[0]
    for k in reversed(range(count)):
        start, end = k * B, (k + 1) * B
        here = w_hi[:, start:end].astype(F32) + w_lo[:, start:end].astype(F32)
        for left, right in ((end + B, points), (end, min(end + B, points))):
            if left >= right:
                continue
            if k < cut:
                rows = slice(left - end, right - end)
                below = head_hi[k, rows, :], head_lo[k, rows, :]
            else:
                rows = slice(left - (cut + 1) * B, right - (cut + 1) * B)
                columns = slice((k - cut) * B, (k - cut + 1) * B)
                below = low_hi[rows, columns], low_lo[rows, columns]
            here = here - product_nn((v_hi[:, left:right], v_mid[:, left:right]), below)
        if k <= cut:
            tri = first_hi[k, B:, :], first_lo[k, B:, :]
        else:
            tri = last_hi[k - cut - 1, B:, :], last_lo[k - cut - 1, B:, :]
        parts = thirds(product_nn(split(here), tri))
        v_hi[:, start:end], v_mid[:, start:end], v_last[:, start:end] = parts
    sensors = perm[...]
    out[...] = dot_nt(v_hi[...], sensors) + (
        dot_nt(v_mid[...], sensors) + dot_nt(v_last[...], sensors)
    )


def solve(factors, perm, w_hi, w_lo):
    return pl.pallas_call(
        solve_kernel,
        out_shape=jax.ShapeDtypeStruct(w_hi.shape, F32),
        in_specs=[vmem()] * (3 + len(factors)),
        out_specs=vmem(),
        scratch_shapes=[pltpu.VMEM(w_hi.shape, BF16)] * 3,
        **limit(10, 4 * 10**9),
        name="solve",
    )(*factors, perm, w_hi, w_lo)


def pivot_block(corner, spare):
    row = lax.broadcasted_iota(jnp.int32, (B, B), 0)
    column = lax.broadcasted_iota(jnp.int32, (B, B), 1)
    corner[...] = corner[...] + jnp.where(row == column, 1.0, 0.0)
    tri, pivots = sweep(rows_from(corner), spare)
    return split(tri), log_sum(pivots) / B


def pivot_kernel(shared, received, other, tri_hi, tri_lo, logs, corner, spare):
    half = B // 2
    start, across = half_of(half)
    corner[pl.ds(start, half), :] = shared[pl.ds(start, half), :] + received[...]
    corner[pl.ds(across, half), :] = shared[pl.ds(across, half), :] + other[...]
    (tri_hi[...], tri_lo[...]), log = pivot_block(corner, spare)
    logs[...] = jnp.broadcast_to(log, logs.shape)


def pivot(depth, shared, received, other):
    tri = jax.ShapeDtypeStruct((2 * B, B), BF16)
    return pl.pallas_call(
        pivot_kernel,
        out_shape=(tri, tri, jax.ShapeDtypeStruct((SUB, B), F32)),
        in_specs=[vmem()] * 3,
        out_specs=(vmem(),) * 3,
        scratch_shapes=[pltpu.VMEM((B, B), F32), spare_rows()],
        **limit(6, 18 * 10**8 if depth == 0 else 5 * 10**8),
        name="pivot",
    )(shared, received, other)


def merge_kernel(depth, levels, extra, *refs):
    shared, tail, received, other, tri_hi, tri_lo, logs = refs[:7]
    next_shared, next_tail = refs[7:9]
    *sends, w_out, tri_out = refs[9:-2]
    merged, below = refs[-2:]
    left = levels - depth
    half = halves(left)[3]
    start, across = half_of(half)
    merged[pl.ds(start, half), :] = shared[pl.ds(B + start, half), :] + received[:half, :]
    merged[pl.ds(across, half), :] = shared[pl.ds(B + across, half), :] + other[...]
    below[...] = tail[...] + received[half:, :]
    left -= 1
    panel = join([merged[: left * B, :], below[:extra, :]], 0)
    both = product_nt(split(panel), (tri_hi[...], tri_lo[...]))
    w_parts = split(both[:, :B])
    m_parts = split(both[:, B:])
    w_out[...] = both[:, :B]
    tri_out[...] = tri_hi[B:, :].astype(F32) + tri_lo[B:, :].astype(F32)
    at = 0
    for entry in range(left):
        top = entry * B
        rows = (left - entry) * B
        change = product_nt(
            tuple(part[top:] for part in m_parts),
            tuple(part[top : top + B] for part in w_parts),
        )
        base = left * B + at
        next_shared[at : at + rows, :] = merged[base : base + rows, :] - change[:rows]
        next_tail[entry * extra : (entry + 1) * extra, :] = (
            below[(entry + 1) * extra : (entry + 2) * extra, :] - change[rows:]
        )
        at += rows
    lane = lax.broadcasted_iota(jnp.int32, (SUB, B), 1)
    next_tail[left * extra :, :] = below[(left + 1) * extra :, :] + jnp.where(
        lane == depth + 1, logs[...], 0.0
    )
    outgoing(next_shared, next_tail, *sends)


def merge(depth, levels, extra, arrived):
    left = levels - depth
    messages = message_shapes(left - 1, extra)
    return pl.pallas_call(
        functools.partial(merge_kernel, depth, levels, extra),
        out_shape=(
            *messages,
            jax.ShapeDtypeStruct(((left - 1) * B + extra, B), F32),
            jax.ShapeDtypeStruct((B, B), F32),
        ),
        in_specs=[vmem()] * 7,
        out_specs=(vmem(),) * (2 + len(messages)),
        scratch_shapes=[
            pltpu.VMEM((halves(left)[1], B), F32),
            pltpu.VMEM((left * extra + SUB, B), F32),
        ],
        **limit(6),
        name="merge",
    )(*arrived)


def finish_kernel(levels, leaf_count, shared, tail, received, solved, out, means, corner, spare):
    extra = out.shape[0]
    corner[...] = shared[...] + received[:B, :]
    tri, log = pivot_block(corner, spare)
    below = tail[...] + received[B:, :]
    target = product_nt(split(below[:extra]), tuple(part[:B] for part in tri))
    coeffs = split(product_nn(split(target), tuple(part[B:] for part in tri)))
    out[...] = solved[B:, :] - product_nn(coeffs, split(solved[:B, :]))
    totals = below[extra:]
    lane = lax.broadcasted_iota(jnp.int32, (SUB, B), 1)
    scale = jnp.zeros((SUB, B), F32)
    for entry in range(levels + 1):
        scale = jnp.where(lane == entry, 2.0**entry / leaf_count, scale)
    totals = totals + jnp.where(lane == levels, log, 0.0)
    means[...] = (totals * scale)[:1, : levels + 1]


def finish(levels, leaf_count, extra, message, solved):
    return pl.pallas_call(
        functools.partial(finish_kernel, levels, leaf_count),
        out_shape=(
            jax.ShapeDtypeStruct((extra, solved.shape[1]), F32),
            jax.ShapeDtypeStruct((1, levels + 1), F32),
        ),
        in_specs=[vmem()] * 4,
        out_specs=(vmem(),) * 2,
        scratch_shapes=[pltpu.VMEM((B, B), F32), spare_rows()],
        **limit(6),
        name="finish",
    )(*message, solved)


def swapped(value, axis, mask):
    pairs = [(source, source ^ mask) for source in range(lax.axis_size(axis))]
    return lax.ppermute(value, axis, pairs)


def exchange(message, depth, left, meanwhile):
    shared, tail, *sends = message
    received = [swapped(send, "leaf", 2**depth) for send in sends]
    received[0], done = lax.optimization_barrier((received[0], meanwhile()))
    if len(sends) == 1:
        return (shared, tail, received[0]), done
    tri = pivot(depth, shared, received[0], swapped(received[0], "rep", 1))
    late, tri = lax.optimization_barrier((received[1], tri))
    other = swapped(late[: halves(left)[3]], "rep", 1)
    return (shared, tail, late, other, *tri), done


def shards(leaf_blocks, generators, rhs, order, ranks):
    levels = generators.shape[0]
    extra = rhs.shape[0]
    cut = leaf_blocks.shape[1] // B // 2 - 1
    pieces = [generators, swapped(generators, "rep", 1)]
    far = [swapped(generators, "rep", mask) for mask in range(2, lax.axis_size("rep"), 2)]
    *factors, logs, rest = head(cut, leaf_blocks)
    far, logs = lax.optimization_barrier((far, logs))
    for arrived in far:
        pieces += [arrived, swapped(arrived, "rep", 1)]
    perm, moved = prepare(rhs, order)
    *message, w_hi, w_lo, a, b, c, d = forward(
        ranks.T, pieces, moved, (*factors, logs, rest)
    )
    factors += [a, b, c, d]
    halves_of = (w_hi, w_lo)
    level = None
    for depth in range(levels):

        def meanwhile():
            rows = halves_of if level is None else reduce(*level, *halves_of)
            return solve(factors, perm, *rows) if depth + 1 == levels else rows

        arrived, halves_of = exchange(message, depth, levels - depth, meanwhile)
        if depth + 1 < levels:
            *message, w_level, tri_level = merge(depth, levels, extra, arrived)
            level = (w_level, tri_level)
    out, means = finish(levels, lax.axis_size("leaf"), extra, arrived, halves_of)
    return (out, means.reshape(levels + 1))


def solution(mesh):
    placed = (
        P("leaf", None),
        P(None, "rep", "leaf"),
        P("rep", "leaf"),
        P("leaf", None),
        P(None, "leaf"),
    )
    return jax.shard_map(
        shards, mesh=mesh, in_specs=placed, out_specs=(P("rep", "leaf"), P()), check_vma=False
    )
```

```python
import functools

import jax
import jax.numpy as jnp
from jax import lax
from jax.experimental import pallas as pl
from jax.experimental.pallas import tpu as pltpu
from jax.sharding import PartitionSpec as P

F32 = jnp.float32
BF16 = jnp.bfloat16
B = 128
SUB = 8


def limit(mebibytes, flops=0):
    return dict(
        compiler_params=pltpu.CompilerParams(vmem_limit_bytes=mebibytes * 2**20),
        cost_estimate=pl.CostEstimate(flops=flops, bytes_accessed=2**20, transcendentals=0),
    )


def vmem():
    return pl.BlockSpec(memory_space=pltpu.VMEM)


def lanes_of(value, lane):
    index = jnp.full((SUB, B), lane, jnp.int32)
    return jnp.take_along_axis(value, index, axis=1, mode="promise_in_bounds")


def row_of(value, row):
    return jnp.broadcast_to(value[row : row + 1, :], (SUB, B))


def sweep(rows, spare):
    lane = lax.broadcasted_iota(jnp.int32, (SUB, B), 1)
    sub = lax.broadcasted_iota(jnp.int32, (SUB, B), 0)
    count = B // SUB
    pivots = jnp.ones((SUB, B), F32)
    rows = list(rows)
    t, rt = [None] * count, [None] * count
    cols = [lanes_of(rows[0], l) for l in range(SUB)]

    def update(group, base, inside, spread):
        weights = [[] for _ in group]
        for l in range(SUB):
            for weight, q in zip(weights, group):
                weight.append(lanes_of(rows[q], base + l))
        for weight, q in zip(weights, group):
            apply(q, inside, spread, weight)

    def apply(q, inside, spread, weight):
        even = jnp.where(inside, 0.0, rows[q]) - weight[0] * spread[0]
        odd = weight[1] * spread[1]
        for l in range(2, SUB, 2):
            even = even - weight[l] * spread[l]
            odd = odd + weight[l + 1] * spread[l + 1]
        rows[q] = even - odd

    for p in range(count):
        base = SUB * p
        inside = (lane >= base) & (lane < base + SUB)
        upto = lane < base + SUB
        panel = jnp.where(inside, jnp.where(lane - base == sub, 1.0, 0.0), rows[p])
        t[p] = jnp.where(upto, panel, 0.0)
        following = p + 1 < count
        ahead = None
        if following:
            first = [lanes_of(rows[p + 1], base + l) for l in range(SUB)]
            below = list(first)
            ahead = [lanes_of(rows[p + 1], base + SUB + l) for l in range(SUB)]
        for j in range(SUB):
            across = {l: row_of(cols[l], j) for l in range(j, SUB)}
            pivots = jnp.where(lane == base + j, across[j], pivots)
            inverse = pltpu.reciprocal(across[j], approx=True)
            scale = jnp.where(sub == j, 1.0 - inverse, cols[j] * inverse)
            for l in range(j + 1, SUB):
                cols[l] = cols[l] - scale * across[l]
            panel = panel - scale * row_of(panel, j)
            if following:
                slot = (p % 2) * SUB + j
                spare[slot, :SUB, :] = below[j]
                factor = below[j] * inverse
                for l in range(SUB):
                    ahead[l] = ahead[l] - factor * spare[slot, pl.ds(l, SUB, stride=0), :]
                for l in range(j + 1, SUB):
                    below[l] = below[l] - factor * across[l]
        rt[p] = jnp.where(upto, panel, 0.0)
        if following:
            spread = [row_of(panel, i) for i in range(SUB)]
            apply(p + 1, inside, spread, first)
            update(list(range(p + 2, min(p + 3, count))), base, inside, spread)
            for q in range(p + 3, count, 3):
                update(list(range(q, min(q + 3, count))), base, inside, spread)
        cols = ahead
    return jnp.concatenate(t + rt, axis=0), pivots


def spare_rows():
    return pltpu.VMEM((2 * SUB, 2 * SUB, B), F32)


def rows_from(ref):
    return [ref[SUB * p : SUB * (p + 1), :B] for p in range(B // SUB)]


def split(value):
    high = value.astype(BF16)
    return high, (value - high.astype(F32)).astype(BF16)


def dot_nt(left, right):
    return lax.dot_general(left, right, (((1,), (1,)), ((), ())), preferred_element_type=F32)


def dot_nn(left, right):
    return lax.dot_general(left, right, (((1,), (0,)), ((), ())), preferred_element_type=F32)


def join(parts, axis):
    return jnp.concatenate(parts, axis=axis)


def product_nt(left, right):
    lh, ll = left
    rh, rl = right
    return dot_nt(join([lh, lh, ll], 1), join([rh, rl, rh], 1))


def product_nn(left, right):
    lh, ll = left
    rh, rl = right
    return dot_nn(join([lh, lh, ll], 1), join([rh, rl, rh], 0))


def log_sum(pivots):
    return jnp.sum(jnp.log(pivots[:1]), axis=1, keepdims=True)


def eliminate_column(panel, corner, tri):
    both = product_nt(split(panel[:B]), tri)
    below, mult = split(both[:, :B]), split(both[:, B:])
    corner = corner - product_nt(mult, below)
    if panel.shape[0] > B:
        both = product_nt(split(panel[B:]), tri)
        below = tuple(join(pair, 0) for pair in zip(below, split(both[:, :B])))
        mult = tuple(join(pair, 0) for pair in zip(mult, split(both[:, B:])))
    return below, mult, [corner[SUB * p : SUB * (p + 1)] for p in range(B // SUB)]


def trail(source, target, mult, below):
    src, src_off = source
    dst, dst_off = target
    size = mult[0].shape[0]
    for col in range(0, size, B):
        change = product_nt(
            tuple(part[col:] for part in mult), tuple(part[col : col + B] for part in below)
        )
        fresh = src[src_off + col : src_off + size, src_off + col : src_off + col + B] - change
        dst[dst_off + col : dst_off + size, dst_off + col : dst_off + col + B] = fresh


def head_kernel(
    cut, blocks, low_hi, low_lo, tri_hi, tri_lo, logs, work, corner, spare, sems
):
    points = work.shape[0]
    whole_copy = pltpu.make_async_copy(blocks, work, sems.at[0])
    first_copy = pltpu.make_async_copy(blocks.at[:B, :B], corner, sems.at[1])
    first_copy.start()
    whole_copy.start()
    first_copy.wait()
    tri, pivots = sweep(rows_from(corner), spare)
    tri_hi[0], tri_lo[0] = split(tri)
    whole_copy.wait()

    def step(k, total):
        below, mult, rows = eliminate_column(
            work[B:, :B], work[B : 2 * B, B : 2 * B], (tri_hi[k], tri_lo[k])
        )
        low_hi[k], low_lo[k] = below
        tri, pivots = sweep(rows, spare)
        tri_hi[k + 1], tri_lo[k + 1] = split(tri)
        trail((work, B), (work, 0), mult, below)
        return total + log_sum(pivots)

    total = lax.fori_loop(0, cut, step, log_sum(pivots))
    logs[...] = jnp.broadcast_to(total, logs.shape)


def head(cut, block):
    points = block.shape[1]
    low = jax.ShapeDtypeStruct((cut, points - B, B), BF16)
    tri = jax.ShapeDtypeStruct((cut + 1, 2 * B, B), BF16)
    return pl.pallas_call(
        functools.partial(head_kernel, cut),
        out_shape=(
            low,
            low,
            tri,
            tri,
            jax.ShapeDtypeStruct((SUB, B), F32),
            jax.ShapeDtypeStruct((points, points), F32),
        ),
        in_specs=[pl.BlockSpec(memory_space=pltpu.HBM)],
        out_specs=(vmem(),) * 6,
        scratch_shapes=[
            pltpu.VMEM((B, B), F32),
            spare_rows(),
            pltpu.SemaphoreType.DMA((2,)),
        ],
        **limit(10),
        name="head",
    )(pltpu.with_memory_space_constraint(block, pltpu.HBM))


def permutation(order_ref, points):
    sensor = lax.broadcasted_iota(jnp.int32, (points, points), 0)
    return jnp.where(sensor == order_ref[...], 1.0, 0.0).astype(BF16)


def thirds(value):
    high = value.astype(BF16)
    rest = value - high.astype(F32)
    mid = rest.astype(BF16)
    return high, mid, (rest - mid.astype(F32)).astype(BF16)


def column_rows(levels, extra, entry):
    return (levels - entry) * B + extra


def halves(levels):
    rest = sum((levels - entry) * B for entry in range(levels)) - B
    if levels > 2:
        return B, rest, B // 2, rest // 2
    return B, rest, B, rest


def half_of(size):
    start = pl.multiple_of((lax.axis_index("rep") % 2) * size, SUB)
    return start, pl.multiple_of(size - start, SUB)


def gram_tiles(levels, extra):
    bottom = levels * B + extra
    tiles = []
    for entry in range(0, levels, 2):
        left, mid, right = entry * B, (entry + 1) * B, (entry + 2) * B
        if entry + 1 < levels:
            tiles += [(left, mid, left, mid), (mid, bottom, left, right)]
        else:
            tiles.append((left, bottom, left, mid))
    return tiles


def prepare_kernel(rhs, order, perm, moved):
    extra, points = rhs.shape
    perm[...] = permutation(order, points)
    parts = dot_nn(join(thirds(rhs[...]), 0), perm[...])
    moved[...] = parts[:extra] + (parts[extra : 2 * extra] + parts[2 * extra :])


def prepare(rhs, order):
    points = rhs.shape[1]
    return pl.pallas_call(
        prepare_kernel,
        out_shape=(
            jax.ShapeDtypeStruct((points, points), BF16),
            jax.ShapeDtypeStruct(rhs.shape, F32),
        ),
        in_specs=[vmem()] * 2,
        out_specs=(vmem(),) * 2,
        **limit(8, 10**9),
        name="prepare",
    )(rhs, order)


def forward_kernel(levels, size, *refs):
    head_hi, head_lo, first_hi, first_lo, logs, before, ranks = refs[:7]
    pieces = refs[7 : 7 + size]
    moved = refs[7 + size]
    *sends, w_hi, w_lo, low_hi, low_lo, last_hi, last_lo = refs[10 + size : -5]
    shared, tail = refs[8 + size : 10 + size]
    work, values, m_hi, m_lo, spare = refs[-5:]
    extra, points = moved.shape
    count = points // B
    cut = head_hi.shape[0]
    quarter = pieces[0].shape[1]
    own = lax.axis_index("rep")
    for level in range(levels):
        limit_here = ranks[:, level : level + 1]
        for shift in range(size):
            first = (own ^ shift) * quarter
            row = lax.broadcasted_iota(jnp.int32, (quarter, points), 0) + first
            at = pl.multiple_of(level * B + first, SUB)
            values[pl.ds(at, quarter), :] = jnp.where(
                row < limit_here, pieces[shift][level], 0.0
            )
    values[levels * B :, :] = moved[...]

    def tri_of(k):
        if k <= cut:
            return first_hi[k], first_lo[k]
        return last_hi[k - cut - 1], last_lo[k - cut - 1]

    def low_of(k, left, right):
        parts = []
        for old, new in ((head_hi, low_hi), (head_lo, low_lo)):
            blocks = [old[j, (k - j - 1) * B : (k - j) * B, :] for j in range(left, min(right, cut))]
            start = max(left, cut)
            if start < right:
                rows = slice((k - cut - 1) * B, (k - cut) * B)
                blocks.append(new[rows, (start - cut) * B : (right - cut) * B])
            parts.append(join(blocks, 1))
        return tuple(parts)

    def advance(k):
        start, end = k * B, (k + 1) * B
        here = values[:, start:end]
        for left, right in ((0, k - 1), (max(k - 1, 0), k)):
            if left < right:
                held = slice(left * B, right * B)
                here = here - product_nt((m_hi[:, held], m_lo[:, held]), low_of(k, left, right))
        both = product_nt(split(here), tri_of(k))
        w_hi[:, start:end], w_lo[:, start:end] = split(both[:, :B])
        m_hi[:, start:end], m_lo[:, start:end] = split(both[:, B:])

    total = logs[:1, :1]
    tiles = gram_tiles(levels, extra)
    sums = [None] * len(tiles)
    done, summed = 0, 0

    def accumulate(stop):
        held = slice(summed * B, stop * B)
        for i, (top, bottom, left, right) in enumerate(tiles):
            piece = product_nt(
                (m_hi[top:bottom, held], m_lo[top:bottom, held]),
                (w_hi[left:right, held], w_lo[left:right, held]),
            )
            sums[i] = piece if sums[i] is None else sums[i] + piece
        return stop

    for at in range(cut, count - 1):
        src = before if at == cut else work
        base = (at - cut) * B
        size_here = points - at * B
        below, mult, rows = eliminate_column(
            src[base + B : base + size_here, base : base + B],
            src[base + B : base + 2 * B, base + B : base + 2 * B],
            tri_of(at),
        )
        low_hi[base:, base : base + B], low_lo[base:, base : base + B] = below
        tri, pivots = sweep(rows, spare)
        last_hi[at - cut], last_lo[at - cut] = split(tri)
        total = total + log_sum(pivots)
        trail((src, base + B), (work, base + B), mult, below)
        goal = min(at + 1, (at - cut + 1) * count // (count - 1 - cut))
        while done < goal:
            advance(done)
            done += 1
        if at + 3 >= count:
            summed = accumulate(done)
    for k in range(done, count):
        advance(k)
    accumulate(count)
    for (top, bottom, left, right), block in zip(tiles, sums):
        for entry in range(left // B, right // B):
            base = sum((levels - i) * B for i in range(entry)) - entry * B
            part = block[:, entry * B - left : (entry + 1) * B - left]
            stop = min(bottom, levels * B)
            shared[base + top : base + stop, :] = part[: stop - top]
            if bottom > stop:
                tail[entry * extra : (entry + 1) * extra, :] = part[stop - top :]
    lane = lax.broadcasted_iota(jnp.int32, (SUB, B), 1)
    tail[levels * extra :, :] = jnp.where(lane == 0, total / points, 0.0)
    outgoing(shared, tail, *sends)


def outgoing(shared, tail, *sends):
    if len(sends) == 1:
        sends[0][:B, :] = shared[...]
        sends[0][B:, :] = tail[...]
        return
    corner, others = sends
    half = others.shape[0] - tail.shape[0]
    if corner.shape[0] == B:
        corner[...] = shared[:B, :]
        others[:half, :] = shared[B:, :]
    else:
        corner[...] = shared[pl.ds(half_of(B // 2)[0], B // 2), :]
        others[:half, :] = shared[pl.ds(B + half_of(half)[0], half), :]
    others[half:, :] = tail[...]


def message_shapes(levels, extra):
    first, rest, half_first, half_rest = halves(levels)
    tail = levels * extra + SUB
    if levels > 1:
        sends = (half_first, half_rest + tail)
    else:
        sends = (first + tail,)
    return [jax.ShapeDtypeStruct((rows, B), F32) for rows in (first + rest, tail, *sends)]


def forward(ranks, pieces, moved, factors):
    levels, _, points = pieces[0].shape
    extra = moved.shape[0]
    rows = levels * B + extra
    count = points // B
    cut = factors[0].shape[0]
    left = (count - 1 - cut) * B
    low = jax.ShapeDtypeStruct((left, left), BF16)
    tri = jax.ShapeDtypeStruct((count - 1 - cut, 2 * B, B), BF16)
    half = jax.ShapeDtypeStruct((rows, points), BF16)
    return pl.pallas_call(
        functools.partial(forward_kernel, levels, len(pieces)),
        out_shape=(*message_shapes(levels, extra), half, half, low, low, tri, tri),
        in_specs=[vmem()] * (8 + len(pieces)),
        out_specs=(vmem(),) * (6 + len(message_shapes(levels, extra))),
        scratch_shapes=[
            pltpu.VMEM((left + B, left + B), F32),
            pltpu.VMEM((rows, points), F32),
            pltpu.VMEM((rows, points), BF16),
            pltpu.VMEM((rows, points), BF16),
            spare_rows(),
        ],
        **limit(16),
        name="forward",
    )(*factors, ranks, *pieces, moved)


def reduce_rows(w_panel, tri, w_hi, w_lo):
    coeffs = split(product_nn(split(w_panel[...]), split(tri[...])))
    rest = w_hi[B:, :].astype(F32) + w_lo[B:, :].astype(F32)
    return split(rest - product_nn(coeffs, (w_hi[:B, :], w_lo[:B, :])))


def reduce_kernel(w_panel, tri, w_hi, w_lo, out_hi, out_lo):
    out_hi[...], out_lo[...] = reduce_rows(w_panel, tri, w_hi, w_lo)


def reduce(w_panel, tri, w_hi, w_lo):
    shape = jax.ShapeDtypeStruct((w_hi.shape[0] - B, w_hi.shape[1]), BF16)
    return pl.pallas_call(
        reduce_kernel,
        out_shape=(shape, shape),
        in_specs=[vmem()] * 4,
        out_specs=(vmem(),) * 2,
        **limit(8, 4 * 10**9),
        name="reduce",
    )(w_panel, tri, w_hi, w_lo)


def solve_blocks(first, last, factors, w_hi, w_lo, v):
    head_hi, head_lo, first_hi, first_lo, low_hi, low_lo, last_hi, last_lo = factors
    points = w_hi.shape[1]
    cut = head_hi.shape[0]
    for k in reversed(range(first, last)):
        start, end = k * B, (k + 1) * B
        here = w_hi[:, start:end].astype(F32) + w_lo[:, start:end].astype(F32)
        for left, right in ((end + B, points), (end, min(end + B, points))):
            if left >= right:
                continue
            if k < cut:
                rows = slice(left - end, right - end)
                below = head_hi[k, rows, :], head_lo[k, rows, :]
            else:
                rows = slice(left - (cut + 1) * B, right - (cut + 1) * B)
                columns = slice((k - cut) * B, (k - cut + 1) * B)
                below = low_hi[rows, columns], low_lo[rows, columns]
            here = here - product_nn((v[0][:, left:right], v[1][:, left:right]), below)
        if k <= cut:
            tri = first_hi[k, B:, :], first_lo[k, B:, :]
        else:
            tri = last_hi[k - cut - 1, B:, :], last_lo[k - cut - 1, B:, :]
        for ref, part in zip(v, thirds(product_nn(split(here), tri))):
            ref[:, start:end] = part


def begin_kernel(ahead, *refs):
    factors, (w_hi, w_lo), v = refs[:8], refs[8:10], refs[10:12]
    points = w_hi.shape[1]
    stop = points - ahead * B
    solve_blocks(stop // B, points // B, factors, w_hi, w_lo, v)
    v[0][:, :stop] = w_hi[:, :stop]
    v[1][:, :stop] = w_lo[:, :stop]


def begin(ahead, factors, w_hi, w_lo):
    return pl.pallas_call(
        functools.partial(begin_kernel, ahead),
        out_shape=(jax.ShapeDtypeStruct(w_hi.shape, BF16),) * 2,
        in_specs=[vmem()] * 10,
        out_specs=(vmem(),) * 2,
        **limit(8, 10**8),
        name="begin",
    )(*factors, w_hi, w_lo)


def solve_kernel(ahead, *refs):
    factors, (perm, w_hi, w_lo, out), v = refs[:8], refs[8:12], refs[12:]
    points = w_hi.shape[1]
    stop = points - ahead * B
    v[0][:, stop:] = w_hi[:, stop:]
    v[1][:, stop:] = w_lo[:, stop:]
    solve_blocks(0, stop // B, factors, w_hi, w_lo, v)
    sensors = perm[...]
    last = dot_nt(v[2][:, :stop], perm[:, :stop])
    out[...] = dot_nt(v[0][...], sensors) + (dot_nt(v[1][...], sensors) + last)


def solve(ahead, factors, perm, w_hi, w_lo):
    return pl.pallas_call(
        functools.partial(solve_kernel, ahead),
        out_shape=jax.ShapeDtypeStruct(w_hi.shape, F32),
        in_specs=[vmem()] * (3 + len(factors)),
        out_specs=vmem(),
        scratch_shapes=[pltpu.VMEM(w_hi.shape, BF16)] * 3,
        **limit(10, 4 * 10**9),
        name="solve",
    )(*factors, perm, w_hi, w_lo)


def pivot_block(corner, spare):
    row = lax.broadcasted_iota(jnp.int32, (B, B), 0)
    column = lax.broadcasted_iota(jnp.int32, (B, B), 1)
    corner[...] = corner[...] + jnp.where(row == column, 1.0, 0.0)
    tri, pivots = sweep(rows_from(corner), spare)
    return split(tri), log_sum(pivots) / B


def add_halves(out, shared, skip, received, other):
    if not other:
        out[...] = shared[skip : skip + out.shape[0], :] + received
        return
    half = out.shape[0] // 2
    start, across = half_of(half)
    out[pl.ds(start, half), :] = shared[pl.ds(skip + start, half), :] + received
    out[pl.ds(across, half), :] = shared[pl.ds(skip + across, half), :] + other[0][...]


def pivot_kernel(shared, received, *refs):
    *other, tri_hi, tri_lo, logs, corner, spare = refs
    add_halves(corner, shared, 0, received[...], other)
    (tri_hi[...], tri_lo[...]), log = pivot_block(corner, spare)
    logs[...] = jnp.broadcast_to(log, logs.shape)


def pivot(depth, shared, *received):
    tri = jax.ShapeDtypeStruct((2 * B, B), BF16)
    return pl.pallas_call(
        pivot_kernel,
        out_shape=(tri, tri, jax.ShapeDtypeStruct((SUB, B), F32)),
        in_specs=[vmem()] * (1 + len(received)),
        out_specs=(vmem(),) * 3,
        scratch_shapes=[pltpu.VMEM((B, B), F32), spare_rows()],
        **limit(6, 18 * 10**8 if depth == 0 else 5 * 10**8),
        name="pivot",
    )(shared, *received)


def merge_kernel(depth, levels, extra, *refs):
    left = levels - depth
    split_up = int(left > 2)
    shared, tail, received = refs[:3]
    other = refs[3 : 3 + split_up]
    tri_hi, tri_lo, logs, next_shared, next_tail = refs[3 + split_up : 8 + split_up]
    *sends, w_out, tri_out = refs[8 + split_up : -2]
    merged, below = refs[-2:]
    half = halves(left)[3]
    add_halves(merged, shared, B, received[:half, :], other)
    below[...] = tail[...] + received[half:, :]
    left -= 1
    panel = join([merged[: left * B, :], below[:extra, :]], 0)
    both = product_nt(split(panel), (tri_hi[...], tri_lo[...]))
    w_parts = split(both[:, :B])
    m_parts = split(both[:, B:])
    w_out[...] = both[:, :B]
    tri_out[...] = tri_hi[B:, :].astype(F32) + tri_lo[B:, :].astype(F32)
    at = 0
    for entry in range(left):
        top = entry * B
        rows = (left - entry) * B
        change = product_nt(
            tuple(part[top:] for part in m_parts),
            tuple(part[top : top + B] for part in w_parts),
        )
        base = left * B + at
        next_shared[at : at + rows, :] = merged[base : base + rows, :] - change[:rows]
        next_tail[entry * extra : (entry + 1) * extra, :] = (
            below[(entry + 1) * extra : (entry + 2) * extra, :] - change[rows:]
        )
        at += rows
    lane = lax.broadcasted_iota(jnp.int32, (SUB, B), 1)
    next_tail[left * extra :, :] = below[(left + 1) * extra :, :] + jnp.where(
        lane == depth + 1, logs[...], 0.0
    )
    outgoing(next_shared, next_tail, *sends)


def merge(depth, levels, extra, arrived):
    left = levels - depth
    messages = message_shapes(left - 1, extra)
    return pl.pallas_call(
        functools.partial(merge_kernel, depth, levels, extra),
        out_shape=(
            *messages,
            jax.ShapeDtypeStruct(((left - 1) * B + extra, B), F32),
            jax.ShapeDtypeStruct((B, B), F32),
        ),
        in_specs=[vmem()] * len(arrived),
        out_specs=(vmem(),) * (2 + len(messages)),
        scratch_shapes=[
            pltpu.VMEM((halves(left)[1], B), F32),
            pltpu.VMEM((left * extra + SUB, B), F32),
        ],
        **limit(6),
        name="merge",
    )(*arrived)


def finish_kernel(levels, leaf_count, shared, tail, received, solved, out, means, corner, spare):
    extra = out.shape[0]
    corner[...] = shared[...] + received[:B, :]
    tri, log = pivot_block(corner, spare)
    below = tail[...] + received[B:, :]
    target = product_nt(split(below[:extra]), tuple(part[:B] for part in tri))
    coeffs = split(product_nn(split(target), tuple(part[B:] for part in tri)))
    out[...] = solved[B:, :] - product_nn(coeffs, split(solved[:B, :]))
    totals = below[extra:]
    lane = lax.broadcasted_iota(jnp.int32, (SUB, B), 1)
    scale = jnp.zeros((SUB, B), F32)
    for entry in range(levels + 1):
        scale = jnp.where(lane == entry, 2.0**entry / leaf_count, scale)
    totals = totals + jnp.where(lane == levels, log, 0.0)
    means[...] = (totals * scale)[:1, : levels + 1]


def finish(levels, leaf_count, extra, message, solved):
    return pl.pallas_call(
        functools.partial(finish_kernel, levels, leaf_count),
        out_shape=(
            jax.ShapeDtypeStruct((extra, solved.shape[1]), F32),
            jax.ShapeDtypeStruct((1, levels + 1), F32),
        ),
        in_specs=[vmem()] * 4,
        out_specs=(vmem(),) * 2,
        scratch_shapes=[pltpu.VMEM((B, B), F32), spare_rows()],
        **limit(6),
        name="finish",
    )(*message, solved)


def swapped(value, axis, mask):
    pairs = [(source, source ^ mask) for source in range(lax.axis_size(axis))]
    return lax.ppermute(value, axis, pairs)


def exchange(message, depth, left, meanwhile):
    shared, tail, *sends = message
    received = [swapped(send, "leaf", 2**depth) for send in sends]
    received[0], done = lax.optimization_barrier((received[0], meanwhile()))
    if len(sends) == 1:
        return (shared, tail, received[0]), done
    if left <= 2:
        return (shared, tail, received[1], *pivot(depth, shared, received[0])), done
    tri = pivot(depth, shared, received[0], swapped(received[0], "rep", 1))
    late, tri = lax.optimization_barrier((received[1], tri))
    other = swapped(late[: halves(left)[3]], "rep", 1)
    return (shared, tail, late, other, *tri), done


def shards(leaf_blocks, generators, rhs, order, ranks):
    levels = generators.shape[0]
    extra = rhs.shape[0]
    cut = leaf_blocks.shape[1] // B // 2 - 1
    pieces = [generators, swapped(generators, "rep", 1)]
    far = [swapped(generators, "rep", mask) for mask in range(2, lax.axis_size("rep"), 2)]
    *factors, logs, rest = head(cut, leaf_blocks)
    far, logs = lax.optimization_barrier((far, logs))
    for arrived in far:
        pieces += [arrived, swapped(arrived, "rep", 1)]
    perm, moved = prepare(rhs, order)
    *message, w_hi, w_lo, a, b, c, d = forward(
        ranks.T, pieces, moved, (*factors, logs, rest)
    )
    factors += [a, b, c, d]
    halves_of = (w_hi, w_lo)
    ahead = leaf_blocks.shape[1] // B // 2
    level = None
    for depth in range(levels):

        def meanwhile():
            if depth == 0:
                rows = begin(ahead, factors, *halves_of)
            else:
                rows = reduce(*level, *halves_of)
            return solve(ahead, factors, perm, *rows) if depth + 1 == levels else rows

        arrived, halves_of = exchange(message, depth, levels - depth, meanwhile)
        if depth + 1 < levels:
            *message, w_level, tri_level = merge(depth, levels, extra, arrived)
            level = (w_level, tri_level)
    out, means = finish(levels, lax.axis_size("leaf"), extra, arrived, halves_of)
    return (out, means.reshape(levels + 1))


def solution(mesh):
    placed = (
        P("leaf", None),
        P(None, "rep", "leaf"),
        P("rep", "leaf"),
        P("leaf", None),
        P(None, "leaf"),
    )
    return jax.shard_map(
        shards, mesh=mesh, in_specs=placed, out_specs=(P("rep", "leaf"), P()), check_vma=False
    )
```

```python
import functools

import jax
import jax.numpy as jnp
from jax import lax
from jax.experimental import pallas as pl
from jax.experimental.pallas import tpu as pltpu
from jax.sharding import PartitionSpec as P

F32 = jnp.float32
BF16 = jnp.bfloat16
B = 128
SUB = 8


def limit(mebibytes, flops=0):
    return dict(
        compiler_params=pltpu.CompilerParams(vmem_limit_bytes=mebibytes * 2**20),
        cost_estimate=pl.CostEstimate(flops=flops, bytes_accessed=2**20, transcendentals=0),
    )


def vmem():
    return pl.BlockSpec(memory_space=pltpu.VMEM)


def lanes_of(value, lane):
    index = jnp.full((SUB, B), lane, jnp.int32)
    return jnp.take_along_axis(value, index, axis=1, mode="promise_in_bounds")


def row_of(value, row):
    return jnp.broadcast_to(value[row : row + 1, :], (SUB, B))


def sweep(rows, spare):
    lane = lax.broadcasted_iota(jnp.int32, (SUB, B), 1)
    sub = lax.broadcasted_iota(jnp.int32, (SUB, B), 0)
    count = B // SUB
    pivots = jnp.ones((SUB, B), F32)
    rows = list(rows)
    t, rt = [None] * count, [None] * count
    cols = [lanes_of(rows[0], l) for l in range(SUB)]

    def update(group, base, inside, spread):
        weights = [[] for _ in group]
        for l in range(SUB):
            for weight, q in zip(weights, group):
                weight.append(lanes_of(rows[q], base + l))
        for weight, q in zip(weights, group):
            apply(q, inside, spread, weight)

    def apply(q, inside, spread, weight):
        even = jnp.where(inside, 0.0, rows[q]) - weight[0] * spread[0]
        odd = weight[1] * spread[1]
        for l in range(2, SUB, 2):
            even = even - weight[l] * spread[l]
            odd = odd + weight[l + 1] * spread[l + 1]
        rows[q] = even - odd

    for p in range(count):
        base = SUB * p
        inside = (lane >= base) & (lane < base + SUB)
        upto = lane < base + SUB
        panel = jnp.where(inside, jnp.where(lane - base == sub, 1.0, 0.0), rows[p])
        t[p] = jnp.where(upto, panel, 0.0)
        following = p + 1 < count
        if following:
            first = [lanes_of(rows[p + 1], base + l) for l in range(SUB)]
            below = list(first)
            start = [lanes_of(rows[p + 1], base + SUB + l) for l in range(SUB)]
            ahead = [None] * SUB
        for j in range(SUB):
            across = {l: row_of(cols[l], j) for l in range(j, SUB)}
            pivots = jnp.where(lane == base + j, across[j], pivots)
            inverse = pltpu.reciprocal(across[j], approx=True)
            scale = jnp.where(sub == j, 1.0 - inverse, cols[j] * inverse)
            for l in range(j + 1, SUB):
                cols[l] = cols[l] - scale * across[l]
            panel = panel - scale * row_of(panel, j)
            if following:
                slot = (p % 2) * SUB + j
                spare[slot, :SUB, :] = below[j]
                factor = below[j] * inverse
                for l in range(SUB):
                    term = factor * spare[slot, pl.ds(l, SUB, stride=0), :]
                    ahead[l] = term if ahead[l] is None else ahead[l] + term
                for l in range(j + 1, SUB):
                    below[l] = below[l] - factor * across[l]
        rt[p] = jnp.where(upto, panel, 0.0)
        if following:
            spread = [row_of(panel, i) for i in range(SUB)]
            apply(p + 1, inside, spread, first)
            update(list(range(p + 2, min(p + 3, count))), base, inside, spread)
            for q in range(p + 3, count, 3):
                update(list(range(q, min(q + 3, count))), base, inside, spread)
            cols = [before - change for before, change in zip(start, ahead)]
    return jnp.concatenate(t + rt, axis=0), pivots


def spare_rows():
    return pltpu.VMEM((2 * SUB, 2 * SUB, B), F32)


def rows_from(ref):
    return [ref[SUB * p : SUB * (p + 1), :B] for p in range(B // SUB)]


def split(value):
    high = value.astype(BF16)
    return high, (value - high.astype(F32)).astype(BF16)


def dot_nt(left, right):
    return lax.dot_general(left, right, (((1,), (1,)), ((), ())), preferred_element_type=F32)


def dot_nn(left, right):
    return lax.dot_general(left, right, (((1,), (0,)), ((), ())), preferred_element_type=F32)


def join(parts, axis):
    return jnp.concatenate(parts, axis=axis)


def product_nt(left, right):
    lh, ll = left
    rh, rl = right
    return dot_nt(join([lh, lh, ll], 1), join([rh, rl, rh], 1))


def product_nn(left, right):
    lh, ll = left
    rh, rl = right
    return dot_nn(join([lh, lh, ll], 1), join([rh, rl, rh], 0))


def log_sum(pivots):
    return jnp.sum(jnp.log(pivots[:1]), axis=1, keepdims=True)


def eliminate_column(panel, corner, tri):
    both = product_nt(split(panel[:B]), tri)
    below, mult = split(both[:, :B]), split(both[:, B:])
    corner = corner - product_nt(mult, below)
    if panel.shape[0] > B:
        both = product_nt(split(panel[B:]), tri)
        below = tuple(join(pair, 0) for pair in zip(below, split(both[:, :B])))
        mult = tuple(join(pair, 0) for pair in zip(mult, split(both[:, B:])))
    return below, mult, [corner[SUB * p : SUB * (p + 1)] for p in range(B // SUB)]


def trail(source, target, mult, below):
    src, src_off = source
    dst, dst_off = target
    size = mult[0].shape[0]
    for col in range(0, size, B):
        change = product_nt(
            tuple(part[col:] for part in mult), tuple(part[col : col + B] for part in below)
        )
        fresh = src[src_off + col : src_off + size, src_off + col : src_off + col + B] - change
        dst[dst_off + col : dst_off + size, dst_off + col : dst_off + col + B] = fresh


def head_kernel(
    cut, blocks, low_hi, low_lo, tri_hi, tri_lo, logs, work, corner, spare, sems
):
    points = work.shape[0]
    whole_copy = pltpu.make_async_copy(blocks, work, sems.at[0])
    first_copy = pltpu.make_async_copy(blocks.at[:B, :B], corner, sems.at[1])
    first_copy.start()
    whole_copy.start()
    first_copy.wait()
    tri, pivots = sweep(rows_from(corner), spare)
    tri_hi[0], tri_lo[0] = split(tri)
    whole_copy.wait()

    def step(k, total):
        below, mult, rows = eliminate_column(
            work[B:, :B], work[B : 2 * B, B : 2 * B], (tri_hi[k], tri_lo[k])
        )
        low_hi[k], low_lo[k] = below
        tri, pivots = sweep(rows, spare)
        tri_hi[k + 1], tri_lo[k + 1] = split(tri)
        trail((work, B), (work, 0), mult, below)
        return total + log_sum(pivots)

    total = lax.fori_loop(0, cut, step, log_sum(pivots))
    logs[...] = jnp.broadcast_to(total, logs.shape)


def head(cut, block):
    points = block.shape[1]
    low = jax.ShapeDtypeStruct((cut, points - B, B), BF16)
    tri = jax.ShapeDtypeStruct((cut + 1, 2 * B, B), BF16)
    return pl.pallas_call(
        functools.partial(head_kernel, cut),
        out_shape=(
            low,
            low,
            tri,
            tri,
            jax.ShapeDtypeStruct((SUB, B), F32),
            jax.ShapeDtypeStruct((points, points), F32),
        ),
        in_specs=[pl.BlockSpec(memory_space=pltpu.HBM)],
        out_specs=(vmem(),) * 6,
        scratch_shapes=[
            pltpu.VMEM((B, B), F32),
            spare_rows(),
            pltpu.SemaphoreType.DMA((2,)),
        ],
        **limit(10),
        name="head",
    )(pltpu.with_memory_space_constraint(block, pltpu.HBM))


def permutation(order_ref, points):
    sensor = lax.broadcasted_iota(jnp.int32, (points, points), 0)
    return jnp.where(sensor == order_ref[...], 1.0, 0.0).astype(BF16)


def thirds(value):
    high = value.astype(BF16)
    rest = value - high.astype(F32)
    mid = rest.astype(BF16)
    return high, mid, (rest - mid.astype(F32)).astype(BF16)


def column_rows(levels, extra, entry):
    return (levels - entry) * B + extra


def halves(levels):
    rest = sum((levels - entry) * B for entry in range(levels)) - B
    if levels > 2:
        return B, rest, B // 2, rest // 2
    return B, rest, B, rest


def half_of(size):
    start = pl.multiple_of((lax.axis_index("rep") % 2) * size, SUB)
    return start, pl.multiple_of(size - start, SUB)


def gram_tiles(levels, extra):
    bottom = levels * B + extra
    tiles = []
    for entry in range(0, levels, 2):
        left, mid, right = entry * B, (entry + 1) * B, (entry + 2) * B
        if entry + 1 < levels:
            tiles += [(left, mid, left, mid), (mid, bottom, left, right)]
        else:
            tiles.append((left, bottom, left, mid))
    return tiles


def prepare_kernel(rhs, order, perm, moved):
    extra, points = rhs.shape
    perm[...] = permutation(order, points)
    parts = dot_nn(join(thirds(rhs[...]), 0), perm[...])
    moved[...] = parts[:extra] + (parts[extra : 2 * extra] + parts[2 * extra :])


def prepare(rhs, order):
    points = rhs.shape[1]
    return pl.pallas_call(
        prepare_kernel,
        out_shape=(
            jax.ShapeDtypeStruct((points, points), BF16),
            jax.ShapeDtypeStruct(rhs.shape, F32),
        ),
        in_specs=[vmem()] * 2,
        out_specs=(vmem(),) * 2,
        **limit(8, 10**9),
        name="prepare",
    )(rhs, order)


def forward_kernel(levels, size, *refs):
    head_hi, head_lo, first_hi, first_lo, logs, before, ranks = refs[:7]
    pieces = refs[7 : 7 + size]
    moved = refs[7 + size]
    *sends, w_hi, w_lo, low_hi, low_lo, last_hi, last_lo = refs[10 + size : -5]
    shared, tail = refs[8 + size : 10 + size]
    work, values, m_hi, m_lo, spare = refs[-5:]
    extra, points = moved.shape
    count = points // B
    cut = head_hi.shape[0]
    quarter = pieces[0].shape[1]
    own = lax.axis_index("rep")
    for level in range(levels):
        limit_here = ranks[:, level : level + 1]
        for shift in range(size):
            first = (own ^ shift) * quarter
            row = lax.broadcasted_iota(jnp.int32, (quarter, points), 0) + first
            at = pl.multiple_of(level * B + first, SUB)
            values[pl.ds(at, quarter), :] = jnp.where(
                row < limit_here, pieces[shift][level], 0.0
            )
    values[levels * B :, :] = moved[...]

    def tri_of(k):
        if k <= cut:
            return first_hi[k], first_lo[k]
        return last_hi[k - cut - 1], last_lo[k - cut - 1]

    def low_of(k, left, right):
        parts = []
        for old, new in ((head_hi, low_hi), (head_lo, low_lo)):
            blocks = [old[j, (k - j - 1) * B : (k - j) * B, :] for j in range(left, min(right, cut))]
            start = max(left, cut)
            if start < right:
                rows = slice((k - cut - 1) * B, (k - cut) * B)
                blocks.append(new[rows, (start - cut) * B : (right - cut) * B])
            parts.append(join(blocks, 1))
        return tuple(parts)

    def advance(k):
        start, end = k * B, (k + 1) * B
        here = values[:, start:end]
        for left, right in ((0, k - 1), (max(k - 1, 0), k)):
            if left < right:
                held = slice(left * B, right * B)
                here = here - product_nt((m_hi[:, held], m_lo[:, held]), low_of(k, left, right))
        both = product_nt(split(here), tri_of(k))
        w_hi[:, start:end], w_lo[:, start:end] = split(both[:, :B])
        m_hi[:, start:end], m_lo[:, start:end] = split(both[:, B:])

    total = logs[:1, :1]
    tiles = gram_tiles(levels, extra)
    sums = [None] * len(tiles)
    done, summed = 0, 0

    def accumulate(stop):
        held = slice(summed * B, stop * B)
        for i, (top, bottom, left, right) in enumerate(tiles):
            piece = product_nt(
                (m_hi[top:bottom, held], m_lo[top:bottom, held]),
                (w_hi[left:right, held], w_lo[left:right, held]),
            )
            sums[i] = piece if sums[i] is None else sums[i] + piece
        return stop

    for at in range(cut, count - 1):
        src = before if at == cut else work
        base = (at - cut) * B
        size_here = points - at * B
        below, mult, rows = eliminate_column(
            src[base + B : base + size_here, base : base + B],
            src[base + B : base + 2 * B, base + B : base + 2 * B],
            tri_of(at),
        )
        low_hi[base:, base : base + B], low_lo[base:, base : base + B] = below
        tri, pivots = sweep(rows, spare)
        last_hi[at - cut], last_lo[at - cut] = split(tri)
        total = total + log_sum(pivots)
        trail((src, base + B), (work, base + B), mult, below)
        goal = min(at + 1, (at - cut + 1) * count // (count - 1 - cut))
        while done < goal:
            advance(done)
            done += 1
        if at + 3 >= count:
            summed = accumulate(done)
    for k in range(done, count):
        advance(k)
    accumulate(count)
    for (top, bottom, left, right), block in zip(tiles, sums):
        for entry in range(left // B, right // B):
            base = sum((levels - i) * B for i in range(entry)) - entry * B
            part = block[:, entry * B - left : (entry + 1) * B - left]
            stop = min(bottom, levels * B)
            shared[base + top : base + stop, :] = part[: stop - top]
            if bottom > stop:
                tail[entry * extra : (entry + 1) * extra, :] = part[stop - top :]
    lane = lax.broadcasted_iota(jnp.int32, (SUB, B), 1)
    tail[levels * extra :, :] = jnp.where(lane == 0, total / points, 0.0)
    outgoing(shared, tail, *sends)


def outgoing(shared, tail, *sends):
    if len(sends) == 1:
        sends[0][:B, :] = shared[...]
        sends[0][B:, :] = tail[...]
        return
    corner, others = sends
    half = others.shape[0] - tail.shape[0]
    if corner.shape[0] == B:
        corner[...] = shared[:B, :]
        others[:half, :] = shared[B:, :]
    else:
        corner[...] = shared[pl.ds(half_of(B // 2)[0], B // 2), :]
        others[:half, :] = shared[pl.ds(B + half_of(half)[0], half), :]
    others[half:, :] = tail[...]


def message_shapes(levels, extra):
    first, rest, half_first, half_rest = halves(levels)
    tail = levels * extra + SUB
    if levels > 1:
        sends = (half_first, half_rest + tail)
    else:
        sends = (first + tail,)
    return [jax.ShapeDtypeStruct((rows, B), F32) for rows in (first + rest, tail, *sends)]


def forward(ranks, pieces, moved, factors):
    levels, _, points = pieces[0].shape
    extra = moved.shape[0]
    rows = levels * B + extra
    count = points // B
    cut = factors[0].shape[0]
    left = (count - 1 - cut) * B
    low = jax.ShapeDtypeStruct((left, left), BF16)
    tri = jax.ShapeDtypeStruct((count - 1 - cut, 2 * B, B), BF16)
    half = jax.ShapeDtypeStruct((rows, points), BF16)
    return pl.pallas_call(
        functools.partial(forward_kernel, levels, len(pieces)),
        out_shape=(*message_shapes(levels, extra), half, half, low, low, tri, tri),
        in_specs=[vmem()] * (8 + len(pieces)),
        out_specs=(vmem(),) * (6 + len(message_shapes(levels, extra))),
        scratch_shapes=[
            pltpu.VMEM((left + B, left + B), F32),
            pltpu.VMEM((rows, points), F32),
            pltpu.VMEM((rows, points), BF16),
            pltpu.VMEM((rows, points), BF16),
            spare_rows(),
        ],
        **limit(16),
        name="forward",
    )(*factors, ranks, *pieces, moved)


def reduce_rows(w_panel, tri, w_hi, w_lo):
    coeffs = split(product_nn(split(w_panel[...]), split(tri[...])))
    rest = w_hi[B:, :].astype(F32) + w_lo[B:, :].astype(F32)
    return split(rest - product_nn(coeffs, (w_hi[:B, :], w_lo[:B, :])))


def reduce_kernel(w_panel, tri, w_hi, w_lo, out_hi, out_lo):
    out_hi[...], out_lo[...] = reduce_rows(w_panel, tri, w_hi, w_lo)


def reduce(w_panel, tri, w_hi, w_lo):
    shape = jax.ShapeDtypeStruct((w_hi.shape[0] - B, w_hi.shape[1]), BF16)
    return pl.pallas_call(
        reduce_kernel,
        out_shape=(shape, shape),
        in_specs=[vmem()] * 4,
        out_specs=(vmem(),) * 2,
        **limit(8, 4 * 10**9),
        name="reduce",
    )(w_panel, tri, w_hi, w_lo)


def solve_blocks(first, last, factors, w_hi, w_lo, v):
    head_hi, head_lo, first_hi, first_lo, low_hi, low_lo, last_hi, last_lo = factors
    points = w_hi.shape[1]
    cut = head_hi.shape[0]
    for k in reversed(range(first, last)):
        start, end = k * B, (k + 1) * B
        here = w_hi[:, start:end].astype(F32) + w_lo[:, start:end].astype(F32)
        for left, right in ((end + B, points), (end, min(end + B, points))):
            if left >= right:
                continue
            if k < cut:
                rows = slice(left - end, right - end)
                below = head_hi[k, rows, :], head_lo[k, rows, :]
            else:
                rows = slice(left - (cut + 1) * B, right - (cut + 1) * B)
                columns = slice((k - cut) * B, (k - cut + 1) * B)
                below = low_hi[rows, columns], low_lo[rows, columns]
            here = here - product_nn((v[0][:, left:right], v[1][:, left:right]), below)
        if k <= cut:
            tri = first_hi[k, B:, :], first_lo[k, B:, :]
        else:
            tri = last_hi[k - cut - 1, B:, :], last_lo[k - cut - 1, B:, :]
        for ref, part in zip(v, thirds(product_nn(split(here), tri))):
            ref[:, start:end] = part


def begin_kernel(ahead, *refs):
    factors, (w_hi, w_lo), v = refs[:8], refs[8:10], refs[10:12]
    points = w_hi.shape[1]
    stop = points - ahead * B
    solve_blocks(stop // B, points // B, factors, w_hi, w_lo, v)
    v[0][:, :stop] = w_hi[:, :stop]
    v[1][:, :stop] = w_lo[:, :stop]


def begin(ahead, factors, w_hi, w_lo):
    return pl.pallas_call(
        functools.partial(begin_kernel, ahead),
        out_shape=(jax.ShapeDtypeStruct(w_hi.shape, BF16),) * 2,
        in_specs=[vmem()] * 10,
        out_specs=(vmem(),) * 2,
        **limit(8, 10**8),
        name="begin",
    )(*factors, w_hi, w_lo)


def solve_kernel(ahead, *refs):
    factors, (perm, w_hi, w_lo, out), v = refs[:8], refs[8:12], refs[12:]
    points = w_hi.shape[1]
    stop = points - ahead * B
    v[0][:, stop:] = w_hi[:, stop:]
    v[1][:, stop:] = w_lo[:, stop:]
    solve_blocks(0, stop // B, factors, w_hi, w_lo, v)
    sensors = perm[...]
    last = dot_nt(v[2][:, :stop], perm[:, :stop])
    out[...] = dot_nt(v[0][...], sensors) + (dot_nt(v[1][...], sensors) + last)


def solve(ahead, factors, perm, w_hi, w_lo):
    return pl.pallas_call(
        functools.partial(solve_kernel, ahead),
        out_shape=jax.ShapeDtypeStruct(w_hi.shape, F32),
        in_specs=[vmem()] * (3 + len(factors)),
        out_specs=vmem(),
        scratch_shapes=[pltpu.VMEM(w_hi.shape, BF16)] * 3,
        **limit(10, 4 * 10**9),
        name="solve",
    )(*factors, perm, w_hi, w_lo)


def pivot_block(corner, spare):
    row = lax.broadcasted_iota(jnp.int32, (B, B), 0)
    column = lax.broadcasted_iota(jnp.int32, (B, B), 1)
    corner[...] = corner[...] + jnp.where(row == column, 1.0, 0.0)
    tri, pivots = sweep(rows_from(corner), spare)
    return split(tri), log_sum(pivots) / B


def add_halves(out, shared, skip, received, other):
    if not other:
        out[...] = shared[skip : skip + out.shape[0], :] + received
        return
    half = out.shape[0] // 2
    start, across = half_of(half)
    out[pl.ds(start, half), :] = shared[pl.ds(skip + start, half), :] + received
    out[pl.ds(across, half), :] = shared[pl.ds(skip + across, half), :] + other[0][...]


def pivot_kernel(shared, received, *refs):
    *other, tri_hi, tri_lo, logs, corner, spare = refs
    add_halves(corner, shared, 0, received[...], other)
    (tri_hi[...], tri_lo[...]), log = pivot_block(corner, spare)
    logs[...] = jnp.broadcast_to(log, logs.shape)


def pivot(depth, shared, *received):
    tri = jax.ShapeDtypeStruct((2 * B, B), BF16)
    return pl.pallas_call(
        pivot_kernel,
        out_shape=(tri, tri, jax.ShapeDtypeStruct((SUB, B), F32)),
        in_specs=[vmem()] * (1 + len(received)),
        out_specs=(vmem(),) * 3,
        scratch_shapes=[pltpu.VMEM((B, B), F32), spare_rows()],
        **limit(6, 18 * 10**8 if depth == 0 else 5 * 10**8),
        name="pivot",
    )(shared, *received)


def merge_kernel(depth, levels, extra, *refs):
    left = levels - depth
    split_up = int(left > 2)
    shared, tail, received = refs[:3]
    other = refs[3 : 3 + split_up]
    tri_hi, tri_lo, logs, next_shared, next_tail = refs[3 + split_up : 8 + split_up]
    *sends, w_out, tri_out = refs[8 + split_up : -2]
    merged, below = refs[-2:]
    half = halves(left)[3]
    add_halves(merged, shared, B, received[:half, :], other)
    below[...] = tail[...] + received[half:, :]
    left -= 1
    panel = join([merged[: left * B, :], below[:extra, :]], 0)
    both = product_nt(split(panel), (tri_hi[...], tri_lo[...]))
    w_parts = split(both[:, :B])
    m_parts = split(both[:, B:])
    w_out[...] = both[:, :B]
    tri_out[...] = tri_hi[B:, :].astype(F32) + tri_lo[B:, :].astype(F32)
    at = 0
    for entry in range(left):
        top = entry * B
        rows = (left - entry) * B
        change = product_nt(
            tuple(part[top:] for part in m_parts),
            tuple(part[top : top + B] for part in w_parts),
        )
        base = left * B + at
        next_shared[at : at + rows, :] = merged[base : base + rows, :] - change[:rows]
        next_tail[entry * extra : (entry + 1) * extra, :] = (
            below[(entry + 1) * extra : (entry + 2) * extra, :] - change[rows:]
        )
        at += rows
    lane = lax.broadcasted_iota(jnp.int32, (SUB, B), 1)
    next_tail[left * extra :, :] = below[(left + 1) * extra :, :] + jnp.where(
        lane == depth + 1, logs[...], 0.0
    )
    outgoing(next_shared, next_tail, *sends)


def merge(depth, levels, extra, arrived):
    left = levels - depth
    messages = message_shapes(left - 1, extra)
    return pl.pallas_call(
        functools.partial(merge_kernel, depth, levels, extra),
        out_shape=(
            *messages,
            jax.ShapeDtypeStruct(((left - 1) * B + extra, B), F32),
            jax.ShapeDtypeStruct((B, B), F32),
        ),
        in_specs=[vmem()] * len(arrived),
        out_specs=(vmem(),) * (2 + len(messages)),
        scratch_shapes=[
            pltpu.VMEM((halves(left)[1], B), F32),
            pltpu.VMEM((left * extra + SUB, B), F32),
        ],
        **limit(6),
        name="merge",
    )(*arrived)


def finish_kernel(levels, leaf_count, shared, tail, received, solved, out, means, corner, spare):
    extra = out.shape[0]
    corner[...] = shared[...] + received[:B, :]
    tri, log = pivot_block(corner, spare)
    below = tail[...] + received[B:, :]
    target = product_nt(split(below[:extra]), tuple(part[:B] for part in tri))
    coeffs = split(product_nn(split(target), tuple(part[B:] for part in tri)))
    out[...] = solved[B:, :] - product_nn(coeffs, split(solved[:B, :]))
    totals = below[extra:]
    lane = lax.broadcasted_iota(jnp.int32, (SUB, B), 1)
    scale = jnp.zeros((SUB, B), F32)
    for entry in range(levels + 1):
        scale = jnp.where(lane == entry, 2.0**entry / leaf_count, scale)
    totals = totals + jnp.where(lane == levels, log, 0.0)
    means[...] = (totals * scale)[:1, : levels + 1]


def finish(levels, leaf_count, extra, message, solved):
    return pl.pallas_call(
        functools.partial(finish_kernel, levels, leaf_count),
        out_shape=(
            jax.ShapeDtypeStruct((extra, solved.shape[1]), F32),
            jax.ShapeDtypeStruct((1, levels + 1), F32),
        ),
        in_specs=[vmem()] * 4,
        out_specs=(vmem(),) * 2,
        scratch_shapes=[pltpu.VMEM((B, B), F32), spare_rows()],
        **limit(6),
        name="finish",
    )(*message, solved)


def swapped(value, axis, mask):
    pairs = [(source, source ^ mask) for source in range(lax.axis_size(axis))]
    return lax.ppermute(value, axis, pairs)


def exchange(message, depth, left, meanwhile):
    shared, tail, *sends = message
    received = [swapped(send, "leaf", 2**depth) for send in sends]
    received[0], done = lax.optimization_barrier((received[0], meanwhile()))
    if len(sends) == 1:
        return (shared, tail, received[0]), done
    if left <= 2:
        return (shared, tail, received[1], *pivot(depth, shared, received[0])), done
    tri = pivot(depth, shared, received[0], swapped(received[0], "rep", 1))
    late, tri = lax.optimization_barrier((received[1], tri))
    other = swapped(late[: halves(left)[3]], "rep", 1)
    return (shared, tail, late, other, *tri), done


def shards(leaf_blocks, generators, rhs, order, ranks):
    levels = generators.shape[0]
    extra = rhs.shape[0]
    cut = leaf_blocks.shape[1] // B // 2 - 1
    pieces = [generators, swapped(generators, "rep", 1)]
    far = [swapped(generators, "rep", mask) for mask in range(2, lax.axis_size("rep"), 2)]
    *factors, logs, rest = head(cut, leaf_blocks)
    far, logs = lax.optimization_barrier((far, logs))
    for arrived in far:
        pieces += [arrived, swapped(arrived, "rep", 1)]
    perm, moved = prepare(rhs, order)
    *message, w_hi, w_lo, a, b, c, d = forward(
        ranks.T, pieces, moved, (*factors, logs, rest)
    )
    factors += [a, b, c, d]
    halves_of = (w_hi, w_lo)
    ahead = leaf_blocks.shape[1] // B // 2
    level = None
    for depth in range(levels):

        def meanwhile():
            if depth == 0:
                rows = begin(ahead, factors, *halves_of)
            else:
                rows = reduce(*level, *halves_of)
            return solve(ahead, factors, perm, *rows) if depth + 1 == levels else rows

        arrived, halves_of = exchange(message, depth, levels - depth, meanwhile)
        if depth + 1 < levels:
            *message, w_level, tri_level = merge(depth, levels, extra, arrived)
            level = (w_level, tri_level)
    out, means = finish(levels, lax.axis_size("leaf"), extra, arrived, halves_of)
    return (out, means.reshape(levels + 1))


def solution(mesh):
    placed = (
        P("leaf", None),
        P(None, "rep", "leaf"),
        P("rep", "leaf"),
        P("leaf", None),
        P(None, "leaf"),
    )
    return jax.shard_map(
        shards, mesh=mesh, in_specs=placed, out_specs=(P("rep", "leaf"), P()), check_vma=False
    )
```
